512 devices in a mesh: gx: 32 (over z, x), gy: 16 (over y, core).
Axes of the slice: x: 4, y: 8, z: 8, core: 2. Of those that a mesh axis runs over, the one named last changes fastest.
Arguments:
- initial: bfloat16 [32, 16, 384, 512], P('gx', 'gy'), may hold values from -500 to 500
- couplings: bfloat16 [32, 16, 5, 384, 384], P('gx', 'gy'), may hold values from -0.125 to 0.125
- frequencies: float32 [32, 16, 384], P('gx', 'gy'), may hold values from 0.5 to 2
- linked: int32 [32, 16, 4], P('gx', 'gy'), may hold values from 0 to 1, as said below
Outputs:
- orthonormal: bfloat16 [32, 16, 384, 512], P('gx', 'gy')
- diag_scale: float32 [512], replicated
The draws below stay inside these ranges and needn't reach their ends.
Inputs may be any that keep to these rules, and one draw needn't show every extreme that they name: `linked`: 1 where the coupling block toward that neighbour is present, else 0.
All inputs are finite; a program needn't handle non-finite values.
Results may differ from the reference program's by a relative error of at most 0.0046.
The reference program's roundings to bfloat16 on the way count: a program that leaves them out, or rounds other values in their place, can miss the bound.
Values may be sent and summed in bfloat16 or wider, within the bound.
No kernel may reach another device: no remote copies, remote signals or barrier semaphores. Data moves between devices by JAX's collectives and lax.ppermute only.
A program may use at most 64 MiB of HBM per device.

```python
import math
import jax
import jax.numpy as jnp
from jax import lax

BS = 384
K = 512
DEGREE = 3
NBX = 32
NBY = 16
ROWS = 196608


def draw_initial(key, part):
    key = jax.random.fold_in(key, 11)
    first_key = jax.random.fold_in(key, 0)
    second_key = jax.random.fold_in(key, 1)
    fourth_key = jax.random.fold_in(key, 3)
    row_scale = jnp.exp(jax.random.uniform(second_key, (NBX, NBY, BS, 1), jnp.float32) * math.log(10.0))
    block_scale = jnp.exp(jax.random.uniform(fourth_key, (NBX, NBY, 1, 1), jnp.float32) * math.log(10.0))
    values = jnp.clip(jax.random.normal(first_key, (NBX, NBY, BS, K), jnp.float32), -5.0, 5.0)
    return (values * row_scale * block_scale).astype(jnp.bfloat16)


def draw_linked(key, part):
    key = jax.random.fold_in(key, 13)
    level = 1 + jnp.arange(NBX, dtype=jnp.int32) * 4 // NBX
    drawn = jax.random.randint(key, (NBX, NBY, 4), 0, 4, dtype=jnp.int32)
    return (drawn < level[:, None, None]).astype(jnp.int32)


def levels(stream_key, dims, shards, low, largest):
    def one(position, blocks):
        heights = jax.random.uniform(jax.random.fold_in(jax.random.fold_in(stream_key, 6), position), (blocks,), jnp.float32, low / len(shards), largest / len(shards))
        return jnp.repeat(jnp.exp(heights), dims[position] // blocks).reshape((-1,) + (1,) * (len(dims) - position - 1))

    factor_of = one(*shards[0])
    for cut in shards[1:]:
        factor_of = factor_of * one(*cut)
    return factor_of


def normal_values(rng, dims, scale, reach, shards=(), held_as=jnp.bfloat16):
    array = jax.random.normal(rng, dims, jnp.float32) * scale
    if len(shards) > 0:
        array = levels(rng, dims, shards, -0.22, 0.18) * array
    return jnp.clip(array, min=-reach, max=reach).astype(held_as)


def setup_inputs(seed: int = 0) -> dict:
    arg_keys = jax.random.split(jax.random.key(seed), 5)
    return {
        "initial": draw_initial(jax.random.fold_in(arg_keys[4], 71), 0),
        "couplings": normal_values(arg_keys[1], (NBX, NBY, 5, BS, BS), (5 * BS) ** -0.5, 0.125, ((0, 32), (1, 16))),
        "frequencies": jnp.clip(jnp.exp(math.log(2.0) - 1.3862944 * jax.random.uniform(arg_keys[2], (NBX, NBY, BS), jnp.float32) ** levels(arg_keys[2], (NBX, NBY, BS), ((0, 32), (1, 16)), -0.2, 0.2)), 0.5, 2.0),
        "linked": draw_linked(jax.random.fold_in(arg_keys[4], 71), 0),
    }


spectrum_center = 1.25
spectrum_scale = 0.5

def apply_row(window, blocks, diagonal, present):
    middle = window[1, 1:-1]
    sources = (window[0, 1:-1], window[2, 1:-1], window[1, :-2], window[1, 2:])
    summed = diagonal[..., None] * middle.astype(jnp.float32)
    summed = summed + jnp.einsum('bij,bjk->bik', blocks[:, 0].astype(jnp.float32), middle.astype(jnp.float32), precision=lax.Precision.HIGHEST)
    for direction in range(4):
        product = jnp.einsum('bij,bjk->bik', blocks[:, direction + 1].astype(jnp.float32), sources[direction].astype(jnp.float32), precision=lax.Precision.HIGHEST)
        summed = summed + present[:, direction, None, None] * product
    return summed

def operate(field, couplings, frequencies, linked):
    padded = jnp.pad(field, ((1, 1), (1, 1), (0, 0), (0, 0)))

    def one_row(row_index):
        window = lax.dynamic_slice_in_dim(padded, row_index, 3, 0)
        blocks = lax.dynamic_index_in_dim(couplings, row_index, 0, False)
        diagonal = lax.dynamic_index_in_dim(frequencies, row_index, 0, False)
        present = lax.dynamic_index_in_dim(linked, row_index, 0, False).astype(jnp.float32)
        return apply_row(window, blocks, diagonal, present)
    return lax.map(one_row, jnp.arange(NBX, dtype=jnp.int32))

def reference(initial, couplings, frequencies, linked):
    previous = initial.astype(jnp.float32)
    current = spectrum_scale * (operate(initial, couplings, frequencies, linked) - spectrum_center * previous)
    for degree_step in range(DEGREE - 1):
        rounded = current.astype(jnp.bfloat16)
        following = 2.0 * spectrum_scale * (operate(rounded, couplings, frequencies, linked) - spectrum_center * rounded.astype(jnp.float32)) - previous
        previous, current = (current, following)
    matrix_rows = current.reshape(-1, K)
    correlation = jnp.dot(matrix_rows.T.astype(jnp.float32), matrix_rows.astype(jnp.float32), precision=lax.Precision.HIGHEST, preferred_element_type=jnp.float32)
    factor = jnp.linalg.cholesky(correlation)
    inverse = jax.scipy.linalg.solve_triangular(factor, jnp.eye(K, dtype=jnp.float32), lower=True)
    root = math.sqrt(ROWS)
    orthonormal = (jnp.dot(matrix_rows.astype(jnp.float32), inverse.T.astype(jnp.float32), precision=lax.Precision.HIGHEST, preferred_element_type=jnp.float32) * root).astype(jnp.bfloat16)
    diag_scale = jnp.diagonal(factor) / root
    return (orthonormal.reshape(NBX, NBY, BS, K), diag_scale)
```

```python
import functools
import math

import jax
import jax.numpy as jnp
from jax import lax
from jax.experimental import pallas as pl
from jax.experimental.pallas import tpu as pltpu
from jax.sharding import Mesh
from jax.sharding import PartitionSpec as P

CENTER = 1.25
SCALE = 0.5
NB = 128
HIGHEST = lax.Precision.HIGHEST
F32 = jnp.float32
VMEM = pl.BlockSpec(memory_space=pltpu.VMEM)
SMEM = pl.BlockSpec(memory_space=pltpu.SMEM)
GX = ("z", "x")
GY = ("y", "c")
CHIPS = ("z", "x", "y")
N_CHIPS = 256
LIMIT = 40 * 2**20


def dot(a, b, dims, precision=None):
    return lax.dot_general(
        a, b, (dims, ((), ())), precision=precision, preferred_element_type=F32
    )


def self_kernel(v_ref, c_ref, w_ref, o_ref):
    v = v_ref[...]
    o_ref[...] = (w_ref[...] - CENTER) * v.astype(F32) + dot(c_ref[0], v, ((1,), (0,)))


def halo_sum(part_ref, c_ref, l_ref, halos):
    total = part_ref[...]
    for d, h in enumerate(halos):
        total = total + l_ref[d] * dot(c_ref[d + 1], h[...], ((1,), (0,)))
    return total


def first_kernel(part_ref, c_ref, l_ref, h0, h1, h2, h3, o_ref, r_ref):
    out = SCALE * halo_sum(part_ref, c_ref, l_ref, (h0, h1, h2, h3))
    o_ref[...] = out
    r_ref[...] = out.astype(jnp.bfloat16)


def middle_kernel(part_ref, c_ref, l_ref, h0, h1, h2, h3, p_ref, r_ref):
    out = 2.0 * SCALE * halo_sum(part_ref, c_ref, l_ref, (h0, h1, h2, h3)) - p_ref[...].astype(F32)
    r_ref[...] = out.astype(jnp.bfloat16)


def last_kernel(part_ref, c_ref, l_ref, h0, h1, h2, h3, p_ref, core_ref, o_ref, keep_ref, send_ref):
    o_ref[...] = 2.0 * SCALE * halo_sum(part_ref, c_ref, l_ref, (h0, h1, h2, h3)) - p_ref[...]
    n = 0
    for i in range(4):
        left = o_ref[:, i * NB : (i + 1) * NB]
        g = dot(left, o_ref[:, : (i + 1) * NB], ((0,), (0,)), HIGHEST)
        for l in range(i + 1):
            block = g[:, l * NB : (l + 1) * NB]
            rows = slice((n % 5) * NB, (n % 5 + 1) * NB)
            mine = core_ref[0] == n // 5

            @pl.when(mine)
            def _():
                keep_ref[rows, :] = block

            @pl.when(jnp.logical_not(mine))
            def _():
                send_ref[rows, :] = block

            n += 1


def shape(*dims, dtype=F32):
    return jax.ShapeDtypeStruct(dims, dtype)


def call(kernel, outs, specs, name, flops, scratch=()):
    return pl.pallas_call(
        kernel,
        out_shape=outs,
        in_specs=specs,
        out_specs=jax.tree.map(lambda _: VMEM, outs),
        scratch_shapes=scratch,
        compiler_params=pltpu.CompilerParams(vmem_limit_bytes=LIMIT),
        cost_estimate=pl.CostEstimate(flops=flops, bytes_accessed=2**21, transcendentals=0),
        name=name,
    )


def lanes(v, k):
    return jnp.broadcast_to(v[:, k : k + 1], (8, NB))


def row(v, i):
    return jnp.broadcast_to(v[i : i + 1, :], (8, NB))


def leaf(a, z_ref, d_ref):
    lane = lax.broadcasted_iota(jnp.int32, (8, NB), 1)
    sub = lax.broadcasted_iota(jnp.int32, (8, NB), 0)
    z = [(lane == sub + 8 * r).astype(F32) for r in range(16)]
    diag = jnp.zeros((8, NB), F32)
    for m in range(16):
        k0 = 8 * m
        cols = [lanes(a[m], k0 + j) for j in range(8)]
        s = {(i, j): row(cols[j], i) for i in range(8) for j in range(i, 8)}
        rb = [row(a[m], j) for j in range(8)]
        zb = [row(z[m], j) for j in range(8)]
        cr = {r: [lanes(a[r], k0 + j) for j in range(8)] for r in range(m + 1, 16)}
        for j in range(8):
            inv = 1.0 / s[j, j]
            for jj in range(j + 1, 8):
                f = s[j, jj] * inv
                for k in range(jj, 8):
                    s[jj, k] = s[jj, k] - f * s[j, k]
                rb[jj] = rb[jj] - f * rb[j]
                zb[jj] = zb[jj] - f * zb[j]
            for r in range(m + 1, 16):
                low = cr[r][j] * inv
                for jj in range(j + 1, 8):
                    cr[r][jj] = cr[r][jj] - low * s[j, jj]
                a[r] = a[r] - low * rb[j]
                z[r] = z[r] - low * zb[j]
            rs = lax.rsqrt(s[j, j])
            z_ref[k0 + j : k0 + j + 1, :] = (zb[j] * rs)[0:1]
            diag = jnp.where(lane == k0 + j, s[j, j] * rs, diag)
    d_ref[...] = diag[0:1]


def finish_kernel(root, mine_ref, other_ref, f_ref, core_ref, o_ref, d_ref, w_ref, z_ref, e_ref):
    n = 0
    for i in range(4):
        for l in range(i + 1):
            rows = slice((n % 5) * NB, (n % 5 + 1) * NB)
            mine = core_ref[0] == n // 5

            @pl.when(mine)
            def _():
                w_ref[l, i * NB : (i + 1) * NB, :] = mine_ref[rows, :]

            @pl.when(jnp.logical_not(mine))
            def _():
                w_ref[l, i * NB : (i + 1) * NB, :] = other_ref[rows, :]

            n += 1
    for l in range(4):
        w_ref[l, 512:, :] = f_ref[:, l * NB : (l + 1) * NB]

    def step(j, carry):
        start = pl.multiple_of(j * NB, NB)
        tiles = [w_ref[j, pl.ds(start + 8 * r, 8), :] for r in range(16)]
        leaf(tiles, z_ref, e_ref)
        d_ref[pl.ds(j, 1), :] = e_ref[...] * (1.0 / root)
        for l in range(4):

            @pl.when(l == j)
            def _():
                lo = l * NB
                w_ref[l, lo:, :] = dot(w_ref[l, lo:, :], z_ref[...], ((1,), (1,)), HIGHEST)

        for l in range(1, 4):

            @pl.when(l > j)
            def _():
                lo = l * NB
                w_ref[l, lo:, :] = w_ref[l, lo:, :] - dot(
                    w_ref[j, lo:, :], w_ref[j, lo : lo + NB, :], ((1,), (1,)), HIGHEST
                )

        return carry

    lax.fori_loop(0, 4, step, 0)
    for l in range(4):
        o_ref[:, l * NB : (l + 1) * NB] = (w_ref[l, 512:, :] * root).astype(jnp.bfloat16)


def shift(v, axes, count, step):
    pairs = [(i, i + step) for i in range(count) if 0 <= i + step < count]
    return lax.ppermute(v, axes, pairs)


def neighbours(v):
    return (
        shift(v, GX, 32, 1),
        shift(v, GX, 32, -1),
        shift(v, GY, 16, 1),
        shift(v, GY, 16, -1),
    )


def swap(v):
    return lax.ppermute(v, "c", [(0, 1), (1, 0)])


def local(initial, couplings, frequencies, linked):
    rows, width = initial.shape[2:]
    v0 = initial[0, 0]
    blocks = couplings[0, 0]
    weights = frequencies[0, 0][:, None]
    present = linked[0, 0].astype(F32)
    core = lax.axis_index("c").astype(jnp.int32)[None]
    full = shape(rows, width)
    half = shape(rows, width, dtype=jnp.bfloat16)
    flops = 2 * rows * rows * width
    own = call(self_kernel, full, [VMEM] * 3, "own_block", flops)
    specs = [VMEM, VMEM, SMEM] + [VMEM] * 4

    part, halos = own(v0, blocks, weights), neighbours(v0)
    x1, r1 = call(first_kernel, (full, half), specs, "first", 4 * flops)(
        part, blocks, present, *halos
    )
    part, halos = own(r1, blocks, weights), neighbours(r1)
    r2 = call(middle_kernel, half, specs + [VMEM], "middle", 4 * flops)(
        part, blocks, present, *halos, v0
    )
    part, halos = own(r2, blocks, weights), neighbours(r2)
    piece = shape(5 * NB, NB)
    filtered, keep, send = call(
        last_kernel, (full, piece, piece), specs + [VMEM, SMEM], "last_and_correlation", 8 * flops
    )(part, blocks, present, *halos, x1, core)

    summed = keep + swap(send)
    share = 5 * NB * NB // N_CHIPS
    got = lax.all_to_all(summed.reshape(N_CHIPS, share), CHIPS, 0, 0, tiled=True)
    total = got.reshape(N_CHIPS, share).sum(0)
    spread = jnp.broadcast_to(total[None], (N_CHIPS, share))
    mine = lax.all_to_all(spread, CHIPS, 0, 0, tiled=True).reshape(5 * NB, NB)
    other = swap(mine)

    root = math.sqrt(rows * 512)
    out, diag = call(
        functools.partial(finish_kernel, root),
        (half, shape(4, NB)),
        [VMEM] * 3 + [SMEM],
        "finish",
        8 * flops,
        (
            pltpu.VMEM((4, width + rows, NB), F32),
            pltpu.VMEM((NB, NB), F32),
            pltpu.VMEM((1, NB), F32),
        ),
    )(mine, other, filtered, core)
    return out[None, None], diag.reshape(width)


def solution(mesh):
    fine = Mesh(mesh.devices.reshape(8, 4, 8, 2), GX + GY)
    in_specs = (
        P(GX, GY, None, None),
        P(GX, GY, None, None, None),
        P(GX, GY, None),
        P(GX, GY, None),
    )
    out_specs = (P(GX, GY, None, None), P())
    return jax.shard_map(local, mesh=fine, in_specs=in_specs, out_specs=out_specs, check_vma=False)
```

```python
import functools
import math

import jax
import jax.numpy as jnp
from jax import lax
from jax.experimental import pallas as pl
from jax.experimental.pallas import tpu as pltpu
from jax.sharding import Mesh
from jax.sharding import PartitionSpec as P

CENTER = 1.25
SCALE = 0.5
NB = 128
HIGHEST = lax.Precision.HIGHEST
F32 = jnp.float32
VMEM = pl.BlockSpec(memory_space=pltpu.VMEM)
SMEM = pl.BlockSpec(memory_space=pltpu.SMEM)
GX = ("z", "x")
GY = ("y", "c")
CHIPS = ("z", "x", "y")
N_CHIPS = 256
LIMIT = 12 * 2**20


def dot(a, b, dims, precision=None):
    return lax.dot_general(
        a, b, (dims, ((), ())), precision=precision, preferred_element_type=F32
    )


def halo_product(c_ref, l_ref, index, h_ref):
    return l_ref[index - 1].astype(F32) * dot(c_ref[index], h_ref[...], ((1,), (0,)))


def own_kernel(v_ref, c_ref, w_ref, o_ref):
    v = v_ref[...]
    o_ref[...] = (w_ref[...] - CENTER) * v.astype(F32) + dot(c_ref[0], v, ((1,), (0,)))


def halo_sum(part_ref, c_ref, l_ref, i_ref, halos):
    total = part_ref[...]
    for d, h in enumerate(halos):
        total = total + halo_product(c_ref, l_ref, i_ref[d], h)
    return total


def first_kernel(part_ref, c_ref, l_ref, i_ref, h0, h1, h2, h3, o_ref, r_ref):
    out = SCALE * halo_sum(part_ref, c_ref, l_ref, i_ref, (h0, h1, h2, h3))
    o_ref[...] = out
    r_ref[...] = out.astype(jnp.bfloat16)


def middle_kernel(part_ref, c_ref, l_ref, i_ref, h0, h1, h2, h3, p_ref, r_ref):
    out = 2.0 * SCALE * halo_sum(part_ref, c_ref, l_ref, i_ref, (h0, h1, h2, h3)) - p_ref[...].astype(F32)
    r_ref[...] = out.astype(jnp.bfloat16)


def pieces(v):
    high = v.astype(jnp.bfloat16)
    rest = v - high.astype(F32)
    middle = rest.astype(jnp.bfloat16)
    return high, middle, (rest - middle.astype(F32)).astype(jnp.bfloat16)


def product(a, b, dims):
    total = dot(a[1], b[1], dims)
    for i, k in ((0, 2), (2, 0), (0, 1), (1, 0), (0, 0)):
        total = total + dot(a[i], b[k], dims)
    return total


def last_kernel(part_ref, c_ref, l_ref, i_ref, h0, h1, h2, h3, p_ref, core_ref, o_ref, keep_ref, send_ref):
    out = 2.0 * SCALE * halo_sum(part_ref, c_ref, l_ref, i_ref, (h0, h1, h2, h3)) - p_ref[...]
    o_ref[...] = out
    right = pieces(out)
    n = 0
    for i in range(4):
        left = pieces(out[:, i * NB : (i + 1) * NB].T)
        g = product(left, [p[:, : (i + 1) * NB] for p in right], ((1,), (0,)))
        for l in range(i + 1):
            block = g[:, l * NB : (l + 1) * NB]
            rows = slice((n % 5) * NB, (n % 5 + 1) * NB)
            mine = core_ref[0] == n // 5

            @pl.when(mine)
            def _():
                keep_ref[rows, :] = block

            @pl.when(jnp.logical_not(mine))
            def _():
                send_ref[rows, :] = block

            n += 1


def shape(*dims, dtype=F32):
    return jax.ShapeDtypeStruct(dims, dtype)


def call(kernel, outs, specs, name, flops, scratch=()):
    return pl.pallas_call(
        kernel,
        out_shape=outs,
        in_specs=specs,
        out_specs=jax.tree.map(lambda _: VMEM, outs),
        scratch_shapes=scratch,
        compiler_params=pltpu.CompilerParams(vmem_limit_bytes=LIMIT),
        cost_estimate=pl.CostEstimate(flops=flops, bytes_accessed=2**21, transcendentals=0),
        name=name,
    )


def lanes(v, k):
    return jnp.broadcast_to(v[:, k : k + 1], (8, NB))


def row(v, i):
    return jnp.broadcast_to(v[i : i + 1, :], (8, NB))


def leaf(a, z_ref, d_ref):
    lane = lax.broadcasted_iota(jnp.int32, (8, NB), 1)
    sub = lax.broadcasted_iota(jnp.int32, (8, NB), 0)
    z = [(lane == sub + 8 * r).astype(F32) for r in range(16)]
    diag = jnp.zeros((8, NB), F32)
    for m in range(16):
        k0 = 8 * m
        cols = [lanes(a[m], k0 + j) for j in range(8)]
        s = {(i, j): row(cols[j], i) for i in range(8) for j in range(i, 8)}
        rb = [row(a[m], j) for j in range(8)]
        zb = [row(z[m], j) for j in range(8)]
        cr = {r: [lanes(a[r], k0 + j) for j in range(8)] for r in range(m + 1, 16)}
        for j in range(8):
            inv = 1.0 / s[j, j]
            for jj in range(j + 1, 8):
                f = s[j, jj] * inv
                for k in range(jj, 8):
                    s[jj, k] = s[jj, k] - f * s[j, k]
                rb[jj] = rb[jj] - f * rb[j]
                zb[jj] = zb[jj] - f * zb[j]
            for r in range(m + 1, 16):
                low = cr[r][j] * inv
                for jj in range(j + 1, 8):
                    cr[r][jj] = cr[r][jj] - low * s[j, jj]
                a[r] = a[r] - low * rb[j]
                z[r] = z[r] - low * zb[j]
            rs = lax.rsqrt(s[j, j])
            z_ref[k0 + j : k0 + j + 1, :] = (zb[j] * rs)[0:1]
            diag = jnp.where(lane == k0 + j, s[j, j] * rs, diag)
    d_ref[...] = diag[0:1]


def finish_kernel(root, mine_ref, other_ref, f_ref, core_ref, o_ref, d_ref, w_ref, z_ref, e_ref):
    n = 0
    for i in range(4):
        for l in range(i + 1):
            rows = slice((n % 5) * NB, (n % 5 + 1) * NB)
            mine = core_ref[0] == n // 5

            @pl.when(mine)
            def _():
                w_ref[l, i * NB : (i + 1) * NB, :] = mine_ref[rows, :]

            @pl.when(jnp.logical_not(mine))
            def _():
                w_ref[l, i * NB : (i + 1) * NB, :] = other_ref[rows, :]

            n += 1
    for l in range(4):
        w_ref[l, 512:, :] = f_ref[:, l * NB : (l + 1) * NB]

    def step(j, carry):
        start = pl.multiple_of(j * NB, NB)
        tiles = [w_ref[j, pl.ds(start + 8 * r, 8), :] for r in range(16)]
        leaf(tiles, z_ref, e_ref)
        d_ref[pl.ds(j, 1), :] = e_ref[...] * (1.0 / root)
        for l in range(4):

            @pl.when(l == j)
            def _():
                lo = l * NB
                w_ref[l, lo:, :] = dot(w_ref[l, lo:, :], z_ref[...], ((1,), (1,)), HIGHEST)

        for l in range(1, 4):

            @pl.when(l > j)
            def _():
                lo = l * NB
                w_ref[l, lo:, :] = w_ref[l, lo:, :] - dot(
                    w_ref[j, lo:, :], w_ref[j, lo : lo + NB, :], ((1,), (1,)), HIGHEST
                )

        return carry

    lax.fori_loop(0, 4, step, 0)
    for l in range(4):
        o_ref[:, l * NB : (l + 1) * NB] = (w_ref[l, 512:, :] * root).astype(jnp.bfloat16)


def exchange(v, axes, count, first):
    pairs = []
    for i in range(first, count - 1, 2):
        pairs += [(i, i + 1), (i + 1, i)]
    return lax.ppermute(v, axes, pairs)


def neighbours(v):
    return (
        exchange(v, GY, 16, 0),
        exchange(v, GY, 16, 1),
        exchange(v, GX, 32, 0),
        exchange(v, GX, 32, 1),
    )


def swap(v):
    return lax.ppermute(v, "c", [(0, 1), (1, 0)])


def local(initial, couplings, frequencies, linked):
    rows, width = initial.shape[2:]
    v0 = initial[0, 0]
    blocks = couplings[0, 0]
    weights = frequencies[0, 0][:, None]
    present = linked[0, 0]
    core = lax.axis_index("c").astype(jnp.int32)
    odd = lax.rem(lax.axis_index("x"), 2).astype(jnp.int32)
    index = jnp.stack([4 - core, 3 + core, 2 - odd, 1 + odd])
    core = core[None]
    full = shape(rows, width)
    half = shape(rows, width, dtype=jnp.bfloat16)
    flops = 2 * rows * rows * width

    own = call(own_kernel, full, [VMEM] * 3, "own_block", flops)

    def operands(v):
        halos = neighbours(v)
        return (own(v, blocks, weights), blocks, present, index, *halos)

    specs = [VMEM, VMEM, SMEM, SMEM] + [VMEM] * 4
    x1, r1 = call(first_kernel, (full, half), specs, "first", 4 * flops)(*operands(v0))
    r2 = call(middle_kernel, half, specs + [VMEM], "middle", 4 * flops)(*operands(r1), v0)
    piece = shape(5 * NB, NB)
    filtered, keep, send = call(
        last_kernel, (full, piece, piece), specs + [VMEM, SMEM], "last_and_correlation", 8 * flops
    )(*operands(r2), x1, core)

    summed = keep + swap(send)
    share = 5 * NB * NB // N_CHIPS
    got = lax.all_to_all(summed.reshape(N_CHIPS, share), CHIPS, 0, 0, tiled=True)
    total = got.reshape(N_CHIPS, share).sum(0)
    spread = jnp.broadcast_to(total[None], (N_CHIPS, share))
    mine = lax.all_to_all(spread, CHIPS, 0, 0, tiled=True).reshape(5 * NB, NB)
    other = swap(mine)

    root = math.sqrt(rows * 512)
    out, diag = call(
        functools.partial(finish_kernel, root),
        (half, shape(4, NB)),
        [VMEM] * 3 + [SMEM],
        "finish",
        8 * flops,
        (
            pltpu.VMEM((4, width + rows, NB), F32),
            pltpu.VMEM((NB, NB), F32),
            pltpu.VMEM((1, NB), F32),
        ),
    )(mine, other, filtered, core)
    return out[None, None], diag.reshape(width)


def solution(mesh):
    fine = Mesh(mesh.devices.reshape(8, 4, 8, 2), GX + GY)
    in_specs = (
        P(GX, GY, None, None),
        P(GX, GY, None, None, None),
        P(GX, GY, None),
        P(GX, GY, None),
    )
    out_specs = (P(GX, GY, None, None), P())
    return jax.shard_map(local, mesh=fine, in_specs=in_specs, out_specs=out_specs, check_vma=False)
```

```python
import functools
import math

import jax
import jax.numpy as jnp
from jax import lax
from jax.experimental import pallas as pl
from jax.experimental.pallas import tpu as pltpu
from jax.sharding import Mesh
from jax.sharding import PartitionSpec as P

CENTER = 1.25
SCALE = 0.5
NB = 128
HIGHEST = lax.Precision.HIGHEST
F32 = jnp.float32
VMEM = pl.BlockSpec(memory_space=pltpu.VMEM)
SMEM = pl.BlockSpec(memory_space=pltpu.SMEM)
GX = ("z", "x")
GY = ("y", "c")
PLANE = ("z", "y")
LIMIT = 12 * 2**20


def dot(a, b, dims, precision=None):
    return lax.dot_general(
        a, b, (dims, ((), ())), precision=precision, preferred_element_type=F32
    )


def halo_product(c_ref, l_ref, index, h_ref):
    return l_ref[index - 1].astype(F32) * dot(c_ref[index], h_ref[...], ((1,), (0,)))


def own_kernel(v_ref, c_ref, w_ref, o_ref):
    v = v_ref[...]
    o_ref[...] = (w_ref[...] - CENTER) * v.astype(F32) + dot(c_ref[0], v, ((1,), (0,)))


def halo_sum(part_ref, c_ref, l_ref, i_ref, halos):
    total = part_ref[...]
    for d, h in enumerate(halos):
        total = total + halo_product(c_ref, l_ref, i_ref[d], h)
    return total


def first_kernel(part_ref, c_ref, l_ref, i_ref, h0, h1, h2, h3, o_ref, r_ref):
    out = SCALE * halo_sum(part_ref, c_ref, l_ref, i_ref, (h0, h1, h2, h3))
    o_ref[...] = out
    r_ref[...] = out.astype(jnp.bfloat16)


def middle_kernel(part_ref, c_ref, l_ref, i_ref, h0, h1, h2, h3, p_ref, r_ref):
    out = 2.0 * SCALE * halo_sum(part_ref, c_ref, l_ref, i_ref, (h0, h1, h2, h3)) - p_ref[...].astype(F32)
    r_ref[...] = out.astype(jnp.bfloat16)


def split(v):
    high = v.astype(jnp.bfloat16).astype(F32)
    rest = v - high
    middle = rest.astype(jnp.bfloat16).astype(F32)
    return high, middle, rest - middle


def pieces(v):
    return [p.astype(jnp.bfloat16) for p in split(v)]


def product(a, b, dims):
    total = dot(a[1], b[1], dims)
    for i, k in ((0, 2), (2, 0), (0, 1), (1, 0), (0, 0)):
        total = total + dot(a[i], b[k], dims)
    return total


def last_kernel(part_ref, c_ref, l_ref, i_ref, h0, h1, h2, h3, p_ref, core_ref, o_ref, keep_ref, send_ref):
    out = 2.0 * SCALE * halo_sum(part_ref, c_ref, l_ref, i_ref, (h0, h1, h2, h3)) - p_ref[...]
    o_ref[...] = out
    right = pieces(out)
    n = 0
    for i in range(4):
        left = pieces(out[:, i * NB : (i + 1) * NB].T)
        g = product(left, [p[:, : (i + 1) * NB] for p in right], ((1,), (0,)))
        for l in range(i + 1):
            block = g[:, l * NB : (l + 1) * NB]
            rows = slice((n % 5) * NB, (n % 5 + 1) * NB)
            mine = core_ref[0] == n // 5

            @pl.when(mine)
            def _():
                keep_ref[rows, :] = block

            @pl.when(jnp.logical_not(mine))
            def _():
                send_ref[rows, :] = block

            n += 1


def shape(*dims, dtype=F32):
    return jax.ShapeDtypeStruct(dims, dtype)


def call(kernel, outs, specs, name, flops, scratch=()):
    return pl.pallas_call(
        kernel,
        out_shape=outs,
        in_specs=specs,
        out_specs=jax.tree.map(lambda _: VMEM, outs),
        scratch_shapes=scratch,
        compiler_params=pltpu.CompilerParams(vmem_limit_bytes=LIMIT),
        cost_estimate=pl.CostEstimate(flops=flops, bytes_accessed=2**21, transcendentals=0),
        name=name,
    )


NEAR = 3


def lanes(v, k):
    return jnp.broadcast_to(v[:, k : k + 1], (8, NB))


def row(ref, i):
    return jnp.broadcast_to(ref[i : i + 1, :], (8, NB))


def leaf(a, z_ref, d_ref, col_buf, a_buf, z_buf, right_buf, left_buf, hook):
    lane = lax.broadcasted_iota(jnp.int32, (8, NB), 1)
    sub = lax.broadcasted_iota(jnp.int32, (8, NB), 0)
    z = [(lane == sub + 8 * r).astype(F32) for r in range(16)]
    diag = jnp.zeros((8, NB), F32)
    for m in range(16):
        k0, p = 8 * m, m % 2
        near = range(m + 1, min(m + 1 + NEAR, 16))
        for j in range(8):
            col_buf[p, j] = lanes(a[m], k0 + j)
        a_buf[p] = a[m]
        z_buf[p] = z[m]
        s = {(i, j): row(col_buf.at[p, j], i) for i in range(8) for j in range(i, 8)}
        rb = [row(a_buf.at[p], j) for j in range(8)]
        zb = [row(z_buf.at[p], j) for j in range(8)]
        cr = {r: [lanes(a[r], k0 + j) for j in range(8)] for r in near}
        for j in range(8):
            inv = 1.0 / s[j, j]
            for jj in range(j + 1, 8):
                f = s[j, jj] * inv
                for k in range(jj, 8):
                    s[jj, k] = s[jj, k] - f * s[j, k]
                rb[jj] = rb[jj] - f * rb[j]
                zb[jj] = zb[jj] - f * zb[j]
            for r in near:
                low = cr[r][j] * inv
                for jj in range(j + 1, 8):
                    cr[r][jj] = cr[r][jj] - low * s[j, jj]
                a[r] = a[r] - low * rb[j]
                z[r] = z[r] - low * zb[j]
            if m + 1 + NEAR < 16:
                right_buf[p, j : j + 1, :NB] = rb[j][0:1]
                right_buf[p, j : j + 1, NB:] = zb[j][0:1]
                left_buf[p, j : j + 1, :] = (rb[j] * inv)[0:1]
            rs = lax.rsqrt(s[j, j])
            z_ref[k0 + j : k0 + j + 1, :] = (zb[j] * rs)[0:1]
            diag = jnp.where(lane == k0 + j, s[j, j] * rs, diag)
        if m + 1 + NEAR < 16:
            lh, lm, ll = split(left_buf[p])
            rh, rm, rl = split(right_buf[p])
            left = jnp.concatenate([lh, lh, lm, lm, lh, ll], 0).astype(jnp.bfloat16)
            right = jnp.concatenate([rh, rm, rh, rm, rl, rh], 0).astype(jnp.bfloat16)
            change = dot(left, right, ((0,), (0,)))
            for r in range(m + 1 + NEAR, 16):
                a[r] = a[r] - change[8 * r : 8 * r + 8, :NB]
                z[r] = z[r] - change[8 * r : 8 * r + 8, NB:]
        hook(m)
    d_ref[...] = diag[0:1]


def finish_kernel(
    root, mine_ref, other_ref, f_ref, core_ref, o_ref, d_ref, w_ref, z_ref, e_ref, *bufs
):
    order = {}
    for i in range(4):
        for l in range(i + 1):
            order[i, l] = len(order)
    stored = set()

    def rows(i):
        return slice(i * NB, (i + 1) * NB)

    def get(i, l):
        if (i, l) in stored:
            return w_ref[l, rows(i), :]
        if i >= 4:
            return f_ref[rows(i - 4), rows(l)]
        n = order[i, l]
        here, there = mine_ref[rows(n % 5), :], other_ref[rows(n % 5), :]
        return jnp.where(core_ref[0] == n // 5, here, there)

    def put(i, l, v):
        w_ref[l, rows(i), :] = v
        stored.add((i, l))

    def panel(i, j):
        v = dot(get(i, j), z_ref[j], ((1,), (1,)), HIGHEST)
        put(i, j, v)
        if i >= 4:
            o_ref[rows(i - 4), rows(j)] = (v * root).astype(jnp.bfloat16)

    def update(i, l, j):
        change = dot(w_ref[j, rows(i), :], w_ref[j, rows(l), :], ((1,), (1,)), HIGHEST)
        put(i, l, get(i, l) - change)

    queue = []

    def hook(_):
        if queue:
            task, where = queue.pop(0)
            task(*where)

    for j in range(4):
        block = get(j, j)
        leaf([block[8 * r : 8 * r + 8] for r in range(16)], z_ref.at[j], e_ref, *bufs, hook)
        d_ref[j : j + 1, :] = e_ref[...] * (1.0 / root)
        while queue:
            hook(j)
        if j < 3:
            panel(j + 1, j)
            update(j + 1, j + 1, j)
        for i in range(j + 2, 4):
            queue.append((panel, (i, j)))
        for i in range(j + 2, 4):
            queue.append((update, (i, j + 1, j)))
        for i in range(j + 2, 4):
            for l in range(j + 2, i + 1):
                queue.append((update, (i, l, j)))
        for i in range(4, 7):
            queue.append((panel, (i, j)))
            for l in range(j + 1, 4):
                queue.append((update, (i, l, j)))
    while queue:
        hook(4)


def exchange(v, axes, count, first):
    pairs = []
    for i in range(first, count - 1, 2):
        pairs += [(i, i + 1), (i + 1, i)]
    return lax.ppermute(v, axes, pairs)


def neighbours(v):
    return (
        exchange(v, GY, 16, 0),
        exchange(v, GY, 16, 1),
        exchange(v, GX, 32, 0),
        exchange(v, GX, 32, 1),
    )


def swap(v):
    return lax.ppermute(v, "c", [(0, 1), (1, 0)])


def local(initial, couplings, frequencies, linked):
    rows, width = initial.shape[2:]
    v0 = initial[0, 0]
    blocks = couplings[0, 0]
    weights = frequencies[0, 0][:, None]
    present = linked[0, 0]
    core = lax.axis_index("c").astype(jnp.int32)
    odd = lax.rem(lax.axis_index("x"), 2).astype(jnp.int32)
    index = jnp.stack([4 - core, 3 + core, 2 - odd, 1 + odd])
    core = core[None]
    full = shape(rows, width)
    half = shape(rows, width, dtype=jnp.bfloat16)
    flops = 2 * rows * rows * width

    own = call(own_kernel, full, [VMEM] * 3, "own_block", flops)

    def operands(v):
        halos = neighbours(v)
        return (own(v, blocks, weights), blocks, present, index, *halos)

    specs = [VMEM, VMEM, SMEM, SMEM] + [VMEM] * 4
    x1, r1 = call(first_kernel, (full, half), specs, "first", 4 * flops)(*operands(v0))
    r2 = call(middle_kernel, half, specs + [VMEM], "middle", 4 * flops)(*operands(r1), v0)
    piece = shape(5 * NB, NB)
    filtered, keep, send = call(
        last_kernel, (full, piece, piece), specs + [VMEM, SMEM], "last_and_correlation", 8 * flops
    )(*operands(r2), x1, core)

    summed = keep + swap(send)
    quarter = 5 * NB // 4
    share = quarter * NB // 64
    part = lax.all_to_all(summed.reshape(4, quarter, NB), "x", 0, 0).sum(0)
    part = lax.all_to_all(part.reshape(64, share), PLANE, 0, 0, tiled=True)
    total = part.reshape(64, share).sum(0)
    part = lax.all_to_all(jnp.broadcast_to(total[None], (64, share)), PLANE, 0, 0, tiled=True)
    part = part.reshape(1, quarter, NB)
    mine = lax.all_to_all(jnp.broadcast_to(part, (4, quarter, NB)), "x", 0, 0)
    mine = mine.reshape(5 * NB, NB)
    other = swap(mine)

    root = math.sqrt(rows * 512)
    out, diag = call(
        functools.partial(finish_kernel, root),
        (half, shape(4, NB)),
        [VMEM] * 3 + [SMEM],
        "finish",
        8 * flops,
        (
            pltpu.VMEM((4, width + rows, NB), F32),
            pltpu.VMEM((4, NB, NB), F32),
            pltpu.VMEM((1, NB), F32),
            pltpu.VMEM((2, 8, 8, NB), F32),
            pltpu.VMEM((2, 8, NB), F32),
            pltpu.VMEM((2, 8, NB), F32),
            pltpu.VMEM((2, 8, 2 * NB), F32),
            pltpu.VMEM((2, 8, NB), F32),
        ),
    )(mine, other, filtered, core)
    return out[None, None], diag.reshape(width)


def solution(mesh):
    fine = Mesh(mesh.devices.reshape(8, 4, 8, 2), GX + GY)
    in_specs = (
        P(GX, GY, None, None),
        P(GX, GY, None, None, None),
        P(GX, GY, None),
        P(GX, GY, None),
    )
    out_specs = (P(GX, GY, None, None), P())
    return jax.shard_map(local, mesh=fine, in_specs=in_specs, out_specs=out_specs, check_vma=False)
```

```python
import functools
import math

import jax
import jax.numpy as jnp
from jax import lax
from jax.experimental import pallas as pl
from jax.experimental.pallas import tpu as pltpu
from jax.sharding import Mesh
from jax.sharding import PartitionSpec as P

CENTER = 1.25
SCALE = 0.5
NB = 128
F32 = jnp.float32
VMEM = pl.BlockSpec(memory_space=pltpu.VMEM)
SMEM = pl.BlockSpec(memory_space=pltpu.SMEM)
GX = ("z", "x")
GY = ("y", "c")
PLANE = ("z", "y")
LIMIT = 12 * 2**20


def dot(a, b, dims):
    return lax.dot_general(a, b, (dims, ((), ())), preferred_element_type=F32)


def halo_sum(c_ref, l_ref, i_ref, halos):
    none = jnp.zeros(c_ref.shape[1:], c_ref.dtype)
    left = []
    for k in range(4):
        index = i_ref[k]
        left.append(jnp.where(l_ref[index - 1] != 0, c_ref[index], none))
    right = jnp.concatenate([h[...] for h in halos], 0)
    return dot(jnp.concatenate(left, 1), right, ((1,), (0,)))


def own_kernel(v_ref, c_ref, w_ref, o_ref):
    v = v_ref[...]
    o_ref[...] = (w_ref[...] - CENTER) * v.astype(F32) + dot(c_ref[0], v, ((1,), (0,)))


def first_kernel(part_ref, c_ref, l_ref, i_ref, h0, h1, h2, h3, o_ref, r_ref):
    out = SCALE * (part_ref[...] + halo_sum(c_ref, l_ref, i_ref, (h0, h1, h2, h3)))
    o_ref[...] = out
    r_ref[...] = out.astype(jnp.bfloat16)


def middle_kernel(part_ref, c_ref, l_ref, i_ref, h0, h1, h2, h3, p_ref, r_ref):
    total = part_ref[...] + halo_sum(c_ref, l_ref, i_ref, (h0, h1, h2, h3))
    r_ref[...] = (2.0 * SCALE * total - p_ref[...].astype(F32)).astype(jnp.bfloat16)


def split(v):
    high = v.astype(jnp.bfloat16).astype(F32)
    rest = v - high
    middle = rest.astype(jnp.bfloat16).astype(F32)
    return high, middle, rest - middle


def stack(parts, axis):
    return jnp.concatenate(parts, axis).astype(jnp.bfloat16)


def left_stack(v, axis):
    high, middle, low = split(v)
    return stack([low, high, middle, middle, high, high], axis)


def right_stack(v, axis):
    high, middle, low = split(v)
    return stack([high, low, middle, high, middle, high], axis)


def last_kernel(part_ref, c_ref, l_ref, i_ref, h0, h1, h2, h3, p_ref, core_ref, *outs):
    o_ref, keep_ref, send_ref, g_ref = outs
    total = part_ref[...] + halo_sum(c_ref, l_ref, i_ref, (h0, h1, h2, h3))
    out = 2.0 * SCALE * total - p_ref[...]
    o_ref[...] = out
    left, right = left_stack(out, 0), right_stack(out, 0)
    for i in (0, 2):
        g = dot(left[:, i * NB : (i + 2) * NB], right[:, : (i + 2) * NB], ((0,), (0,)))
        for r in range(i, i + 2):
            for l in range(r + 1):
                n = r * (r + 1) // 2 + l
                block = g[(r - i) * NB : (r - i + 1) * NB, l * NB : (l + 1) * NB]
                g_ref[n * NB : (n + 1) * NB, :] = block
    count = 5 * NB
    core = core_ref[0]
    keep_ref[...] = g_ref[pl.ds(pl.multiple_of(core * count, NB), count), :]
    send_ref[...] = g_ref[pl.ds(pl.multiple_of((1 - core) * count, NB), count), :]


def shape(*dims, dtype=F32):
    return jax.ShapeDtypeStruct(dims, dtype)


def call(kernel, outs, specs, name, flops, scratch=()):
    return pl.pallas_call(
        kernel,
        out_shape=outs,
        in_specs=specs,
        out_specs=jax.tree.map(lambda _: VMEM, outs),
        scratch_shapes=scratch,
        compiler_params=pltpu.CompilerParams(vmem_limit_bytes=LIMIT),
        cost_estimate=pl.CostEstimate(flops=flops, bytes_accessed=2**21, transcendentals=0),
        name=name,
    )


NEAR = 3


def lanes(v, k):
    return jnp.broadcast_to(v[:, k : k + 1], (8, NB))


def row(ref, i):
    return jnp.broadcast_to(ref[i : i + 1, :], (8, NB))


def leaf(a, z_ref, d_ref, col_buf, next_buf, a_buf, z_buf, right_buf, left_buf, hook):
    lane = lax.broadcasted_iota(jnp.int32, (8, NB), 1)
    sub = lax.broadcasted_iota(jnp.int32, (8, NB), 0)
    z = [(lane == sub + 8 * r).astype(F32) for r in range(16)]
    diag = jnp.zeros((8, NB), F32)
    for m in range(16):
        k0, p = 8 * m, m % 2
        near = range(m + 1, min(m + 1 + NEAR, 16))
        if m == 0:
            cols = [lanes(a[0], j) for j in range(8)]
        for j in range(8):
            col_buf[p, j] = cols[j]
        a_buf[p] = a[m]
        z_buf[p] = z[m]
        s = {(i, j): row(col_buf.at[p, j], i) for i in range(8) for j in range(i, 8)}
        rb = [row(a_buf.at[p], j) for j in range(8)]
        zb = [row(z_buf.at[p], j) for j in range(8)]
        cr = {r: [lanes(a[r], k0 + j) for j in range(8)] for r in near}
        if m < 15:
            cols = [lanes(a[m + 1], k0 + 8 + j) for j in range(8)]
        for j in range(8):
            inv = 1.0 / s[j, j]
            for jj in range(j + 1, 8):
                f = s[j, jj] * inv
                for k in range(jj, 8):
                    s[jj, k] = s[jj, k] - f * s[j, k]
                rb[jj] = rb[jj] - f * rb[j]
                zb[jj] = zb[jj] - f * zb[j]
            for r in near:
                low = cr[r][j] * inv
                if r == m + 1:
                    next_buf[p, j] = cr[r][j]
                    for jj in range(8):
                        cols[jj] = cols[jj] - low * row(next_buf.at[p, j], jj)
                for jj in range(j + 1, 8):
                    cr[r][jj] = cr[r][jj] - low * s[j, jj]
                a[r] = a[r] - low * rb[j]
                z[r] = z[r] - low * zb[j]
            if m + 1 + NEAR < 16:
                right_buf[p, j : j + 1, :NB] = rb[j][0:1]
                right_buf[p, j : j + 1, NB:] = zb[j][0:1]
                left_buf[p, j : j + 1, :] = (rb[j] * inv)[0:1]
            rs = lax.rsqrt(s[j, j])
            z_ref[k0 + j : k0 + j + 1, :] = (zb[j] * rs)[0:1]
            diag = jnp.where(lane == k0 + j, s[j, j] * rs, diag)
        if m + 1 + NEAR < 16:
            lo = 8 * (m + 1 + NEAR) // 16 * 16
            across = lax.broadcasted_iota(jnp.int32, (NB - lo, NB), 1)
            down = lax.broadcasted_iota(jnp.int32, (NB - lo, NB), 0)
            unit = (across == down + lo).astype(F32).astype(jnp.bfloat16)
            left = dot(unit, left_stack(left_buf[p], 0), ((1,), (1,))).astype(jnp.bfloat16)
            change = dot(left, right_stack(right_buf[p], 0), ((1,), (0,)))
            for r in range(m + 1 + NEAR, 16):
                at = slice(8 * r - lo, 8 * r - lo + 8)
                a[r] = a[r] - change[at, :NB]
                z[r] = z[r] - change[at, NB:]
        hook(m)
    d_ref[...] = diag[0:1]


def finish_kernel(
    root, mine_ref, other_ref, f_ref, core_ref, o_ref, d_ref, w_ref, z_ref, e_ref, *bufs
):
    order = {}
    for i in range(4):
        for l in range(i + 1):
            order[i, l] = len(order)
    stored = set()

    def rows(i):
        return slice(i * NB, (i + 1) * NB)

    def get(i, l):
        if (i, l) in stored:
            return w_ref[l, rows(i), :]
        if i >= 4:
            return f_ref[rows(i - 4), rows(l)]
        n = order[i, l]
        here, there = mine_ref[rows(n % 5), :], other_ref[rows(n % 5), :]
        return jnp.where(core_ref[0] == n // 5, here, there)

    def put(i, l, v):
        w_ref[l, rows(i), :] = v
        stored.add((i, l))

    def product(a, b):
        return dot(left_stack(a, 1), right_stack(b, 1), ((1,), (1,)))

    def panel(i, j):
        v = product(get(i, j), z_ref[j])
        put(i, j, v)
        if i >= 4:
            o_ref[rows(i - 4), rows(j)] = (v * root).astype(jnp.bfloat16)

    def update(i, l, j):
        put(i, l, get(i, l) - product(w_ref[j, rows(i), :], w_ref[j, rows(l), :]))

    queue = []

    def hook(_):
        if queue:
            task, where = queue.pop(0)
            task(*where)

    for j in range(4):
        block = get(j, j)
        leaf([block[8 * r : 8 * r + 8] for r in range(16)], z_ref.at[j], e_ref, *bufs, hook)
        d_ref[j : j + 1, :] = e_ref[...] * (1.0 / root)
        while queue:
            hook(j)
        if j < 3:
            panel(j + 1, j)
            update(j + 1, j + 1, j)
        for i in range(j + 2, 4):
            queue.append((panel, (i, j)))
        for i in range(j + 2, 4):
            queue.append((update, (i, j + 1, j)))
        for i in range(j + 2, 4):
            for l in range(j + 2, i + 1):
                queue.append((update, (i, l, j)))
        for i in range(4, 7):
            queue.append((panel, (i, j)))
            for l in range(j + 1, 4):
                queue.append((update, (i, l, j)))
    while queue:
        hook(4)


def exchange(v, axes, count, first):
    pairs = []
    for i in range(first, count - 1, 2):
        pairs += [(i, i + 1), (i + 1, i)]
    return lax.ppermute(v, axes, pairs)


def neighbours(v):
    return (
        exchange(v, GY, 16, 0),
        exchange(v, GY, 16, 1),
        exchange(v, GX, 32, 0),
        exchange(v, GX, 32, 1),
    )


def swap(v):
    return lax.ppermute(v, "c", [(0, 1), (1, 0)])


def local(initial, couplings, frequencies, linked):
    rows, width = initial.shape[2:]
    v0 = initial[0, 0]
    blocks = couplings[0, 0]
    weights = frequencies[0, 0][:, None]
    present = linked[0, 0]
    core = lax.axis_index("c").astype(jnp.int32)
    odd = lax.rem(lax.axis_index("x"), 2).astype(jnp.int32)
    index = jnp.stack([4 - core, 3 + core, 2 - odd, 1 + odd])
    core = core[None]
    full = shape(rows, width)
    half = shape(rows, width, dtype=jnp.bfloat16)
    flops = 2 * rows * rows * width

    own = call(own_kernel, full, [VMEM] * 3, "own_block", flops)

    specs = [VMEM] * 2 + [SMEM] * 2 + [VMEM] * 4

    def operands(v):
        halos = neighbours(v)
        return (own(v, blocks, weights), blocks, present, index, *halos)

    x1, r1 = call(first_kernel, (full, half), specs, "first", 4 * flops)(*operands(v0))
    r2 = call(middle_kernel, half, specs + [VMEM], "middle", 4 * flops)(*operands(r1), v0)
    piece = shape(5 * NB, NB)
    filtered, keep, send = call(
        last_kernel,
        (full, piece, piece),
        specs + [VMEM, SMEM],
        "last_and_correlation",
        8 * flops,
        (pltpu.VMEM((10 * NB, NB), F32),),
    )(*operands(r2), x1, core)

    summed = keep + swap(send)
    quarter = 5 * NB // 4
    share = quarter * NB // 64
    part = lax.all_to_all(summed.reshape(4, quarter, NB), "x", 0, 0).sum(0)
    part = lax.all_to_all(part.reshape(64, share), PLANE, 0, 0, tiled=True)
    total = part.reshape(64, share).sum(0)
    part = lax.all_to_all(jnp.broadcast_to(total[None], (64, share)), PLANE, 0, 0, tiled=True)
    part = part.reshape(1, quarter, NB)
    mine = lax.all_to_all(jnp.broadcast_to(part, (4, quarter, NB)), "x", 0, 0)
    mine = mine.reshape(5 * NB, NB)
    other = swap(mine)

    root = math.sqrt(rows * 512)
    out, diag = call(
        functools.partial(finish_kernel, root),
        (half, shape(4, NB)),
        [VMEM] * 3 + [SMEM],
        "finish",
        8 * flops,
        (
            pltpu.VMEM((4, width + rows, NB), F32),
            pltpu.VMEM((4, NB, NB), F32),
            pltpu.VMEM((1, NB), F32),
            pltpu.VMEM((2, 8, 8, NB), F32),
            pltpu.VMEM((2, 8, 8, NB), F32),
            pltpu.VMEM((2, 8, NB), F32),
            pltpu.VMEM((2, 8, NB), F32),
            pltpu.VMEM((2, 8, 2 * NB), F32),
            pltpu.VMEM((2, 8, NB), F32),
        ),
    )(mine, other, filtered, core)
    return out[None, None], diag.reshape(width)


def solution(mesh):
    fine = Mesh(mesh.devices.reshape(8, 4, 8, 2), GX + GY)
    in_specs = (
        P(GX, GY, None, None),
        P(GX, GY, None, None, None),
        P(GX, GY, None),
        P(GX, GY, None),
    )
    out_specs = (P(GX, GY, None, None), P())
    return jax.shard_map(local, mesh=fine, in_specs=in_specs, out_specs=out_specs, check_vma=False)
```

```python
import functools
import math

import jax
import jax.numpy as jnp
from jax import lax
from jax.experimental import pallas as pl
from jax.experimental.pallas import tpu as pltpu
from jax.sharding import Mesh
from jax.sharding import PartitionSpec as P

CENTER = 1.25
SCALE = 0.5
NB = 128
F32 = jnp.float32
VMEM = pl.BlockSpec(memory_space=pltpu.VMEM)
SMEM = pl.BlockSpec(memory_space=pltpu.SMEM)
GX = ("z", "x")
GY = ("y", "c")
LIMIT = 12 * 2**20


def dot(a, b, dims):
    return lax.dot_general(a, b, (dims, ((), ())), preferred_element_type=F32)


def halo_sum(c_ref, l_ref, i_ref, halos):
    none = jnp.zeros(c_ref.shape[1:], c_ref.dtype)
    left = []
    for k in range(4):
        index = i_ref[k]
        left.append(jnp.where(l_ref[index - 1] != 0, c_ref[index], none))
    right = jnp.concatenate([h[...] for h in halos], 0)
    return dot(jnp.concatenate(left, 1), right, ((1,), (0,)))


def own_kernel(v_ref, c_ref, w_ref, o_ref):
    v = v_ref[...]
    o_ref[...] = (w_ref[...] - CENTER) * v.astype(F32) + dot(c_ref[0], v, ((1,), (0,)))


def first_kernel(part_ref, c_ref, l_ref, i_ref, h0, h1, h2, h3, o_ref, r_ref):
    out = SCALE * (part_ref[...] + halo_sum(c_ref, l_ref, i_ref, (h0, h1, h2, h3)))
    o_ref[...] = out
    r_ref[...] = out.astype(jnp.bfloat16)


def middle_kernel(part_ref, c_ref, l_ref, i_ref, h0, h1, h2, h3, p_ref, r_ref):
    total = part_ref[...] + halo_sum(c_ref, l_ref, i_ref, (h0, h1, h2, h3))
    r_ref[...] = (2.0 * SCALE * total - p_ref[...].astype(F32)).astype(jnp.bfloat16)


def split(v):
    high = v.astype(jnp.bfloat16).astype(F32)
    rest = v - high
    middle = rest.astype(jnp.bfloat16).astype(F32)
    return high, middle, rest - middle


def stack(parts, axis):
    return jnp.concatenate(parts, axis).astype(jnp.bfloat16)


def left_stack(v, axis):
    high, middle, low = split(v)
    return stack([low, high, middle, middle, high, high], axis)


def right_stack(v, axis):
    high, middle, low = split(v)
    return stack([high, low, middle, high, middle, high], axis)


def last_kernel(part_ref, c_ref, l_ref, i_ref, h0, h1, h2, h3, p_ref, core_ref, *outs):
    o_ref, keep_ref, send_ref, g_ref = outs
    total = part_ref[...] + halo_sum(c_ref, l_ref, i_ref, (h0, h1, h2, h3))
    out = 2.0 * SCALE * total - p_ref[...]
    o_ref[...] = out
    left, right = left_stack(out, 0), right_stack(out, 0)
    for i in (0, 2):
        g = dot(left[:, i * NB : (i + 2) * NB], right[:, : (i + 2) * NB], ((0,), (0,)))
        for r in range(i, i + 2):
            for l in range(r + 1):
                n = r * (r + 1) // 2 + l
                block = g[(r - i) * NB : (r - i + 1) * NB, l * NB : (l + 1) * NB]
                g_ref[n * NB : (n + 1) * NB, :] = block
    count = 5 * NB
    core = core_ref[0]
    keep_ref[...] = g_ref[pl.ds(pl.multiple_of(core * count, NB), count), :]
    send_ref[...] = g_ref[pl.ds(pl.multiple_of((1 - core) * count, NB), count), :]


def shape(*dims, dtype=F32):
    return jax.ShapeDtypeStruct(dims, dtype)


def call(kernel, outs, specs, name, flops, scratch=()):
    return pl.pallas_call(
        kernel,
        out_shape=outs,
        in_specs=specs,
        out_specs=jax.tree.map(lambda _: VMEM, outs),
        scratch_shapes=scratch,
        compiler_params=pltpu.CompilerParams(vmem_limit_bytes=LIMIT),
        cost_estimate=pl.CostEstimate(flops=flops, bytes_accessed=2**21, transcendentals=0),
        name=name,
    )


NEAR = 3


def lanes(v, k):
    return jnp.broadcast_to(v[:, k : k + 1], (8, NB))


def row(ref, i):
    return jnp.broadcast_to(ref[i : i + 1, :], (8, NB))


def leaf(a, z_ref, d_ref, col_buf, next_buf, a_buf, z_buf, right_buf, left_buf, hook):
    lane = lax.broadcasted_iota(jnp.int32, (8, NB), 1)
    sub = lax.broadcasted_iota(jnp.int32, (8, NB), 0)
    z = [(lane == sub + 8 * r).astype(F32) for r in range(16)]
    diag = jnp.zeros((8, NB), F32)
    for m in range(16):
        k0, p = 8 * m, m % 2
        near = range(m + 1, min(m + 1 + NEAR, 16))
        if m == 0:
            cols = [lanes(a[0], j) for j in range(8)]
        for j in range(8):
            col_buf[p, j] = cols[j]
        a_buf[p] = a[m]
        z_buf[p] = z[m]
        s = {(i, j): row(col_buf.at[p, j], i) for i in range(8) for j in range(i, 8)}
        rb = [row(a_buf.at[p], j) for j in range(8)]
        zb = [row(z_buf.at[p], j) for j in range(8)]
        cr = {r: [lanes(a[r], k0 + j) for j in range(8)] for r in near}
        if m < 15:
            cols = [lanes(a[m + 1], k0 + 8 + j) for j in range(8)]
        for j in range(8):
            inv = 1.0 / s[j, j]
            for jj in range(j + 1, 8):
                f = s[j, jj] * inv
                for k in range(jj, 8):
                    s[jj, k] = s[jj, k] - f * s[j, k]
                rb[jj] = rb[jj] - f * rb[j]
                zb[jj] = zb[jj] - f * zb[j]
            for r in near:
                low = cr[r][j] * inv
                if r == m + 1:
                    next_buf[p, j] = cr[r][j]
                    for jj in range(8):
                        cols[jj] = cols[jj] - low * row(next_buf.at[p, j], jj)
                for jj in range(j + 1, 8):
                    cr[r][jj] = cr[r][jj] - low * s[j, jj]
                a[r] = a[r] - low * rb[j]
                z[r] = z[r] - low * zb[j]
            if m + 1 + NEAR < 16:
                right_buf[p, j : j + 1, :NB] = rb[j][0:1]
                right_buf[p, j : j + 1, NB:] = zb[j][0:1]
                left_buf[p, j : j + 1, :] = (rb[j] * inv)[0:1]
            rs = lax.rsqrt(s[j, j])
            z_ref[k0 + j : k0 + j + 1, :] = (zb[j] * rs)[0:1]
            diag = jnp.where(lane == k0 + j, s[j, j] * rs, diag)
        if m + 1 + NEAR < 16:
            lo = 8 * (m + 1 + NEAR) // 16 * 16
            across = lax.broadcasted_iota(jnp.int32, (NB - lo, NB), 1)
            down = lax.broadcasted_iota(jnp.int32, (NB - lo, NB), 0)
            unit = (across == down + lo).astype(F32).astype(jnp.bfloat16)
            left = dot(unit, left_stack(left_buf[p], 0), ((1,), (1,))).astype(jnp.bfloat16)
            change = dot(left, right_stack(right_buf[p], 0), ((1,), (0,)))
            for r in range(m + 1 + NEAR, 16):
                at = slice(8 * r - lo, 8 * r - lo + 8)
                a[r] = a[r] - change[at, :NB]
                z[r] = z[r] - change[at, NB:]
        hook(m)
    d_ref[...] = diag[0:1]


def finish_kernel(
    root, mine_ref, other_ref, f_ref, core_ref, o_ref, d_ref, w_ref, z_ref, e_ref, *bufs
):
    order = {}
    for i in range(4):
        for l in range(i + 1):
            order[i, l] = len(order)
    stored = set()

    def rows(i):
        return slice(i * NB, (i + 1) * NB)

    def get(i, l):
        if (i, l) in stored:
            return w_ref[l, rows(i), :]
        if i >= 4:
            return f_ref[rows(i - 4), rows(l)]
        n = order[i, l]
        here, there = mine_ref[rows(n % 5), :], other_ref[rows(n % 5), :]
        return jnp.where(core_ref[0] == n // 5, here, there)

    def put(i, l, v):
        w_ref[l, rows(i), :] = v
        stored.add((i, l))

    def product(a, b):
        return dot(left_stack(a, 1), right_stack(b, 1), ((1,), (1,)))

    def panel(i, j):
        v = product(get(i, j), z_ref[j])
        put(i, j, v)
        if i >= 4:
            o_ref[rows(i - 4), rows(j)] = (v * root).astype(jnp.bfloat16)

    def update(i, l, j):
        put(i, l, get(i, l) - product(w_ref[j, rows(i), :], w_ref[j, rows(l), :]))

    queue = []

    def hook(_):
        if queue:
            task, where = queue.pop(0)
            task(*where)

    for j in range(4):
        block = get(j, j)
        leaf([block[8 * r : 8 * r + 8] for r in range(16)], z_ref.at[j], e_ref, *bufs, hook)
        d_ref[j : j + 1, :] = e_ref[...] * (1.0 / root)
        while queue:
            hook(j)
        if j < 3:
            panel(j + 1, j)
            update(j + 1, j + 1, j)
        for i in range(j + 2, 4):
            queue.append((panel, (i, j)))
        for i in range(j + 2, 4):
            queue.append((update, (i, j + 1, j)))
        for i in range(j + 2, 4):
            for l in range(j + 2, i + 1):
                queue.append((update, (i, l, j)))
        for i in range(4, 7):
            queue.append((panel, (i, j)))
            for l in range(j + 1, 4):
                queue.append((update, (i, l, j)))
    while queue:
        hook(4)


def exchange(v, axes, count, first):
    pairs = []
    for i in range(first, count - 1, 2):
        pairs += [(i, i + 1), (i + 1, i)]
    return lax.ppermute(v, axes, pairs)


def neighbours(v):
    return (
        exchange(v, GY, 16, 0),
        exchange(v, GY, 16, 1),
        exchange(v, GX, 32, 0),
        exchange(v, GX, 32, 1),
    )


def swap(v):
    return lax.ppermute(v, "c", [(0, 1), (1, 0)])


def local(initial, couplings, frequencies, linked):
    rows, width = initial.shape[2:]
    v0 = initial[0, 0]
    blocks = couplings[0, 0]
    weights = frequencies[0, 0][:, None]
    present = linked[0, 0]
    core = lax.axis_index("c").astype(jnp.int32)
    odd = lax.rem(lax.axis_index("x"), 2).astype(jnp.int32)
    index = jnp.stack([4 - core, 3 + core, 2 - odd, 1 + odd])
    core = core[None]
    full = shape(rows, width)
    half = shape(rows, width, dtype=jnp.bfloat16)
    flops = 2 * rows * rows * width

    own = call(own_kernel, full, [VMEM] * 3, "own_block", flops)

    specs = [VMEM] * 2 + [SMEM] * 2 + [VMEM] * 4

    def operands(v):
        halos = neighbours(v)
        return (own(v, blocks, weights), blocks, present, index, *halos)

    x1, r1 = call(first_kernel, (full, half), specs, "first", 4 * flops)(*operands(v0))
    r2 = call(middle_kernel, half, specs + [VMEM], "middle", 4 * flops)(*operands(r1), v0)
    piece = shape(5 * NB, NB)
    filtered, keep, send = call(
        last_kernel,
        (full, piece, piece),
        specs + [VMEM, SMEM],
        "last_and_correlation",
        8 * flops,
        (pltpu.VMEM((10 * NB, NB), F32),),
    )(*operands(r2), x1, core)

    summed = keep + swap(send)
    share = 5 * NB * NB // 32
    part = lax.all_to_all(summed.reshape(32, share), GX, 0, 0, tiled=True)
    part = part.reshape(32, share).sum(0).reshape(1, share // NB, NB)
    part = lax.all_to_all(jnp.broadcast_to(part, (8, share // NB, NB)), "y", 0, 0)
    total = part.sum(0).reshape(1, share)
    mine = lax.all_to_all(jnp.broadcast_to(total, (32, share)), GX, 0, 0, tiled=True)
    mine = mine.reshape(5 * NB, NB)
    other = swap(mine)

    root = math.sqrt(rows * 512)
    out, diag = call(
        functools.partial(finish_kernel, root),
        (half, shape(4, NB)),
        [VMEM] * 3 + [SMEM],
        "finish",
        8 * flops,
        (
            pltpu.VMEM((4, width + rows, NB), F32),
            pltpu.VMEM((4, NB, NB), F32),
            pltpu.VMEM((1, NB), F32),
            pltpu.VMEM((2, 8, 8, NB), F32),
            pltpu.VMEM((2, 8, 8, NB), F32),
            pltpu.VMEM((2, 8, NB), F32),
            pltpu.VMEM((2, 8, NB), F32),
            pltpu.VMEM((2, 8, 2 * NB), F32),
            pltpu.VMEM((2, 8, NB), F32),
        ),
    )(mine, other, filtered, core)
    return out[None, None], diag.reshape(width)


def solution(mesh):
    fine = Mesh(mesh.devices.reshape(8, 4, 8, 2), GX + GY)
    in_specs = (
        P(GX, GY, None, None),
        P(GX, GY, None, None, None),
        P(GX, GY, None),
        P(GX, GY, None),
    )
    out_specs = (P(GX, GY, None, None), P())
    return jax.shard_map(local, mesh=fine, in_specs=in_specs, out_specs=out_specs, check_vma=False)
```

```python
import functools
import math

import jax
import jax.numpy as jnp
from jax import lax
from jax.experimental import pallas as pl
from jax.experimental.pallas import tpu as pltpu
from jax.sharding import Mesh
from jax.sharding import PartitionSpec as P

CENTER = 1.25
SCALE = 0.5
NB = 128
F32 = jnp.float32
VMEM = pl.BlockSpec(memory_space=pltpu.VMEM)
SMEM = pl.BlockSpec(memory_space=pltpu.SMEM)
GX = ("z", "x")
GY = ("y", "c")
LIMIT = 12 * 2**20
PART = 4 * NB + 32
PLACES = {(1, 0): (0, 1), (2, 0): (0, 2), (3, 0): (0, 3), (2, 1): (1, 1), (3, 1): (1, 2), (3, 2): (1, 3)}


def iotas():
    return [lax.broadcasted_iota(jnp.int32, (NB, NB), d) for d in (0, 1)]


def dot(a, b, dims):
    return lax.dot_general(a, b, (dims, ((), ())), preferred_element_type=F32)


def halo_sum(c_ref, l_ref, i_ref, halos):
    none = jnp.zeros(c_ref.shape[1:], c_ref.dtype)
    left = []
    for k in range(4):
        index = i_ref[k]
        left.append(jnp.where(l_ref[index - 1] != 0, c_ref[index], none))
    right = jnp.concatenate([h[...] for h in halos], 0)
    return dot(jnp.concatenate(left, 1), right, ((1,), (0,)))


def own_kernel(v_ref, c_ref, w_ref, o_ref):
    v = v_ref[...]
    o_ref[...] = (w_ref[...] - CENTER) * v.astype(F32) + dot(c_ref[0], v, ((1,), (0,)))


def first_kernel(part_ref, c_ref, l_ref, i_ref, h0, h1, h2, h3, o_ref, r_ref):
    out = SCALE * (part_ref[...] + halo_sum(c_ref, l_ref, i_ref, (h0, h1, h2, h3)))
    o_ref[...] = out
    r_ref[...] = out.astype(jnp.bfloat16)


def middle_kernel(part_ref, c_ref, l_ref, i_ref, h0, h1, h2, h3, p_ref, r_ref):
    total = part_ref[...] + halo_sum(c_ref, l_ref, i_ref, (h0, h1, h2, h3))
    r_ref[...] = (2.0 * SCALE * total - p_ref[...].astype(F32)).astype(jnp.bfloat16)


def split(v):
    high = v.astype(jnp.bfloat16).astype(F32)
    rest = v - high
    middle = rest.astype(jnp.bfloat16).astype(F32)
    return high, middle, rest - middle


def stack(parts, axis):
    return jnp.concatenate(parts, axis).astype(jnp.bfloat16)


def left_stack(v, axis):
    high, middle, low = split(v)
    return stack([low, high, middle, middle, high, high], axis)


def right_stack(v, axis):
    high, middle, low = split(v)
    return stack([high, low, middle, high, middle, high], axis)


def last_kernel(part_ref, c_ref, l_ref, i_ref, h0, h1, h2, h3, p_ref, core_ref, *outs):
    o_ref, keep_ref, send_ref, g_ref = outs
    total = part_ref[...] + halo_sum(c_ref, l_ref, i_ref, (h0, h1, h2, h3))
    out = 2.0 * SCALE * total - p_ref[...]
    o_ref[...] = out
    left, right = left_stack(out, 0), right_stack(out, 0)
    down, across = iotas()
    for i in (0, 2):
        g = dot(left[:, i * NB : (i + 2) * NB], right[:, : (i + 2) * NB], ((0,), (0,)))

        def block(r, l):
            return g[(r - i) * NB : (r - i + 1) * NB, l * NB : (l + 1) * NB]

        start = i // 2 * PART
        second = block(i + 1, i + 1)
        g_ref[start : start + NB, :] = jnp.where(down >= across, block(i, i), second)
        tail = jnp.sum(jnp.where(down == across, second, 0.0), 0, keepdims=True)
        g_ref[start + 4 * NB : start + PART, :] = jnp.broadcast_to(tail, (PART - 4 * NB, NB))
        for (r, l), (part, n) in PLACES.items():
            if r in (i, i + 1):
                at = part * PART + n * NB
                g_ref[at : at + NB, :] = block(r, l)
    core = core_ref[0]
    keep_ref[...] = g_ref[pl.ds(pl.multiple_of(core * PART, 8), PART), :]
    send_ref[...] = g_ref[pl.ds(pl.multiple_of((1 - core) * PART, 8), PART), :]


def shape(*dims, dtype=F32):
    return jax.ShapeDtypeStruct(dims, dtype)


def call(kernel, outs, specs, name, flops, scratch=()):
    return pl.pallas_call(
        kernel,
        out_shape=outs,
        in_specs=specs,
        out_specs=jax.tree.map(lambda _: VMEM, outs),
        scratch_shapes=scratch,
        compiler_params=pltpu.CompilerParams(vmem_limit_bytes=LIMIT),
        cost_estimate=pl.CostEstimate(flops=flops, bytes_accessed=2**21, transcendentals=0),
        name=name,
    )


NEAR = 3


def lanes(v, k):
    return jnp.broadcast_to(v[:, k : k + 1], (8, NB))


def row(ref, i):
    return jnp.broadcast_to(ref[i : i + 1, :], (8, NB))


def leaf(a, z_ref, d_ref, col_buf, next_buf, a_buf, z_buf, right_buf, left_buf, hook):
    lane = lax.broadcasted_iota(jnp.int32, (8, NB), 1)
    sub = lax.broadcasted_iota(jnp.int32, (8, NB), 0)
    z = [(lane == sub + 8 * r).astype(F32) for r in range(16)]
    diag = jnp.zeros((8, NB), F32)
    for m in range(16):
        k0, p = 8 * m, m % 2
        near = range(m + 1, min(m + 1 + NEAR, 16))
        if m == 0:
            cols = [lanes(a[0], j) for j in range(8)]
        for j in range(8):
            col_buf[p, j] = cols[j]
        a_buf[p] = a[m]
        z_buf[p] = z[m]
        s = {(i, j): row(col_buf.at[p, j], i) for i in range(8) for j in range(i, 8)}
        rb = [row(a_buf.at[p], j) for j in range(8)]
        zb = [row(z_buf.at[p], j) for j in range(8)]
        cr = {r: [lanes(a[r], k0 + j) for j in range(8)] for r in near}
        if m < 15:
            cols = [lanes(a[m + 1], k0 + 8 + j) for j in range(8)]
        for j in range(8):
            inv = 1.0 / s[j, j]
            for jj in range(j + 1, 8):
                f = s[j, jj] * inv
                for k in range(jj, 8):
                    s[jj, k] = s[jj, k] - f * s[j, k]
                rb[jj] = rb[jj] - f * rb[j]
                zb[jj] = zb[jj] - f * zb[j]
            for r in near:
                low = cr[r][j] * inv
                if r == m + 1:
                    next_buf[p, j] = cr[r][j]
                    for jj in range(8):
                        cols[jj] = cols[jj] - low * row(next_buf.at[p, j], jj)
                for jj in range(j + 1, 8):
                    cr[r][jj] = cr[r][jj] - low * s[j, jj]
                a[r] = a[r] - low * rb[j]
                z[r] = z[r] - low * zb[j]
            if m + 1 + NEAR < 16:
                right_buf[p, j : j + 1, :NB] = rb[j][0:1]
                right_buf[p, j : j + 1, NB:] = zb[j][0:1]
                left_buf[p, j : j + 1, :] = (rb[j] * inv)[0:1]
            rs = lax.rsqrt(s[j, j])
            z_ref[k0 + j : k0 + j + 1, :] = (zb[j] * rs)[0:1]
            diag = jnp.where(lane == k0 + j, s[j, j] * rs, diag)
        if m + 1 + NEAR < 16:
            lo = 8 * (m + 1 + NEAR) // 16 * 16
            across = lax.broadcasted_iota(jnp.int32, (NB - lo, NB), 1)
            down = lax.broadcasted_iota(jnp.int32, (NB - lo, NB), 0)
            unit = (across == down + lo).astype(F32).astype(jnp.bfloat16)
            left = dot(unit, left_stack(left_buf[p], 0), ((1,), (1,))).astype(jnp.bfloat16)
            change = dot(left, right_stack(right_buf[p], 0), ((1,), (0,)))
            for r in range(m + 1 + NEAR, 16):
                at = slice(8 * r - lo, 8 * r - lo + 8)
                a[r] = a[r] - change[at, :NB]
                z[r] = z[r] - change[at, NB:]
        hook(m)
    d_ref[...] = diag[0:1]


def finish_kernel(
    root, mine_ref, other_ref, f_ref, core_ref, o_ref, d_ref, w_ref, z_ref, e_ref, *bufs
):
    stored = set()

    def rows(i):
        return slice(i * NB, (i + 1) * NB)

    def get(i, l):
        if (i, l) in stored:
            return w_ref[l, rows(i), :]
        if i >= 4:
            return f_ref[rows(i - 4), rows(l)]
        if i != l:
            part, n = PLACES[i, l]
            return given(part, slice(n * NB, (n + 1) * NB))
        both = given(i // 2, slice(0, NB))
        if i % 2 == 0:
            return jnp.where(down >= across, both, both.T)
        tail = given(i // 2, slice(4 * NB, 4 * NB + 8))[0:1]
        return jnp.where(down == across, tail, jnp.where(down < across, both, both.T))

    def given(part, at):
        return jnp.where(core_ref[0] == part, mine_ref[at, :], other_ref[at, :])

    down, across = iotas()

    def put(i, l, v):
        w_ref[l, rows(i), :] = v
        stored.add((i, l))

    def product(a, b):
        return dot(left_stack(a, 1), right_stack(b, 1), ((1,), (1,)))

    def panel(i, j):
        v = product(get(i, j), z_ref[j])
        put(i, j, v)
        if i >= 4:
            o_ref[rows(i - 4), rows(j)] = (v * root).astype(jnp.bfloat16)

    def update(i, l, j):
        put(i, l, get(i, l) - product(w_ref[j, rows(i), :], w_ref[j, rows(l), :]))

    queue = []

    def hook(_):
        if queue:
            task, where = queue.pop(0)
            task(*where)

    for j in range(4):
        block = get(j, j)
        leaf([block[8 * r : 8 * r + 8] for r in range(16)], z_ref.at[j], e_ref, *bufs, hook)
        d_ref[j : j + 1, :] = e_ref[...] * (1.0 / root)
        while queue:
            hook(j)
        if j < 3:
            panel(j + 1, j)
            update(j + 1, j + 1, j)
        for i in range(j + 2, 4):
            queue.append((panel, (i, j)))
        for i in range(j + 2, 4):
            queue.append((update, (i, j + 1, j)))
        for i in range(j + 2, 4):
            for l in range(j + 2, i + 1):
                queue.append((update, (i, l, j)))
        for i in range(4, 7):
            queue.append((panel, (i, j)))
            for l in range(j + 1, 4):
                queue.append((update, (i, l, j)))
    while queue:
        hook(4)


def exchange(v, axes, count, first):
    pairs = []
    for i in range(first, count - 1, 2):
        pairs += [(i, i + 1), (i + 1, i)]
    return lax.ppermute(v, axes, pairs)


def neighbours(v):
    return (
        exchange(v, GY, 16, 0),
        exchange(v, GY, 16, 1),
        exchange(v, GX, 32, 0),
        exchange(v, GX, 32, 1),
    )


def swap(v):
    return lax.ppermute(v, "c", [(0, 1), (1, 0)])


def local(initial, couplings, frequencies, linked):
    rows, width = initial.shape[2:]
    v0 = initial[0, 0]
    blocks = couplings[0, 0]
    weights = frequencies[0, 0][:, None]
    present = linked[0, 0]
    core = lax.axis_index("c").astype(jnp.int32)
    odd = lax.rem(lax.axis_index("x"), 2).astype(jnp.int32)
    index = jnp.stack([4 - core, 3 + core, 2 - odd, 1 + odd])
    core = core[None]
    full = shape(rows, width)
    half = shape(rows, width, dtype=jnp.bfloat16)
    flops = 2 * rows * rows * width

    own = call(own_kernel, full, [VMEM] * 3, "own_block", flops)

    specs = [VMEM] * 2 + [SMEM] * 2 + [VMEM] * 4

    def operands(v):
        halos = neighbours(v)
        return (own(v, blocks, weights), blocks, present, index, *halos)

    x1, r1 = call(first_kernel, (full, half), specs, "first", 4 * flops)(*operands(v0))
    r2 = call(middle_kernel, half, specs + [VMEM], "middle", 4 * flops)(*operands(r1), v0)
    piece = shape(PART, NB)
    filtered, keep, send = call(
        last_kernel,
        (full, piece, piece),
        specs + [VMEM, SMEM],
        "last_and_correlation",
        8 * flops,
        (pltpu.VMEM((2 * PART, NB), F32),),
    )(*operands(r2), x1, core)

    summed = keep + swap(send)
    share = PART * NB // 32
    part = lax.all_to_all(summed.reshape(32, share), GX, 0, 0, tiled=True)
    part = part.reshape(32, share).sum(0).reshape(1, share // NB, NB)
    part = lax.all_to_all(jnp.broadcast_to(part, (8, share // NB, NB)), "y", 0, 0)
    total = part.sum(0).reshape(1, share)
    mine = lax.all_to_all(jnp.broadcast_to(total, (32, share)), GX, 0, 0, tiled=True)
    mine = mine.reshape(PART, NB)
    other = swap(mine)

    root = math.sqrt(rows * 512)
    out, diag = call(
        functools.partial(finish_kernel, root),
        (half, shape(4, NB)),
        [VMEM] * 3 + [SMEM],
        "finish",
        8 * flops,
        (
            pltpu.VMEM((4, width + rows, NB), F32),
            pltpu.VMEM((4, NB, NB), F32),
            pltpu.VMEM((1, NB), F32),
            pltpu.VMEM((2, 8, 8, NB), F32),
            pltpu.VMEM((2, 8, 8, NB), F32),
            pltpu.VMEM((2, 8, NB), F32),
            pltpu.VMEM((2, 8, NB), F32),
            pltpu.VMEM((2, 8, 2 * NB), F32),
            pltpu.VMEM((2, 8, NB), F32),
        ),
    )(mine, other, filtered, core)
    return out[None, None], diag.reshape(width)


def solution(mesh):
    fine = Mesh(mesh.devices.reshape(8, 4, 8, 2), GX + GY)
    in_specs = (
        P(GX, GY, None, None),
        P(GX, GY, None, None, None),
        P(GX, GY, None),
        P(GX, GY, None),
    )
    out_specs = (P(GX, GY, None, None), P())
    return jax.shard_map(local, mesh=fine, in_specs=in_specs, out_specs=out_specs, check_vma=False)
```

```python
import functools
import math

import jax
import jax.numpy as jnp
from jax import lax
from jax.experimental import pallas as pl
from jax.experimental.pallas import tpu as pltpu
from jax.sharding import Mesh
from jax.sharding import PartitionSpec as P

CENTER = 1.25
SCALE = 0.5
NB = 128
F32 = jnp.float32
VMEM = pl.BlockSpec(memory_space=pltpu.VMEM)
SMEM = pl.BlockSpec(memory_space=pltpu.SMEM)
GX = ("z", "x")
GY = ("y", "c")
LIMIT = 12 * 2**20
PART = 4 * NB + 32
PLACES = {(1, 0): (0, 1), (2, 0): (0, 2), (3, 0): (0, 3), (2, 1): (1, 1), (3, 1): (1, 2), (3, 2): (1, 3)}


def iotas():
    return [lax.broadcasted_iota(jnp.int32, (NB, NB), d) for d in (0, 1)]


def dot(a, b, dims):
    return lax.dot_general(a, b, (dims, ((), ())), preferred_element_type=F32)


def wide_kernel(c_ref, l_ref, i_ref, x_ref, y_ref):
    none = jnp.zeros(c_ref.shape[1:], c_ref.dtype)
    for k in range(4):
        index = i_ref[k]
        at = slice(k % 2 * none.shape[1], (k % 2 + 1) * none.shape[1])
        (x_ref if k < 2 else y_ref)[:, at] = jnp.where(l_ref[index - 1] != 0, c_ref[index], none)


def halo_sum(part_ref, wide_ref, h0, h1):
    halos = jnp.concatenate([h0[...], h1[...]], 0)
    return part_ref[...] + dot(wide_ref[...], halos, ((1,), (0,)))


def own_kernel(v_ref, c_ref, w_ref, o_ref):
    v = v_ref[...]
    o_ref[...] = (w_ref[...] - CENTER) * v.astype(F32) + dot(c_ref[0], v, ((1,), (0,)))


def x_kernel(part_ref, wide_ref, h0, h1, o_ref):
    o_ref[...] = halo_sum(part_ref, wide_ref, h0, h1)


def first_kernel(part_ref, wide_ref, h0, h1, o_ref, r_ref):
    out = SCALE * halo_sum(part_ref, wide_ref, h0, h1)
    o_ref[...] = out
    r_ref[...] = out.astype(jnp.bfloat16)


def middle_kernel(part_ref, wide_ref, h0, h1, p_ref, r_ref):
    total = halo_sum(part_ref, wide_ref, h0, h1)
    r_ref[...] = (2.0 * SCALE * total - p_ref[...].astype(F32)).astype(jnp.bfloat16)


def split(v):
    high = v.astype(jnp.bfloat16).astype(F32)
    rest = v - high
    middle = rest.astype(jnp.bfloat16).astype(F32)
    return high, middle, rest - middle


def stack(parts, axis):
    return jnp.concatenate(parts, axis).astype(jnp.bfloat16)


def left_stack(v, axis):
    high, middle, low = split(v)
    return stack([low, high, middle, middle, high, high], axis)


def right_stack(v, axis):
    high, middle, low = split(v)
    return stack([high, low, middle, high, middle, high], axis)


def last_kernel(part_ref, wide_ref, h0, h1, p_ref, core_ref, o_ref, keep_ref, send_ref, g_ref):
    out = 2.0 * SCALE * halo_sum(part_ref, wide_ref, h0, h1) - p_ref[...]
    o_ref[...] = out
    left, right = left_stack(out, 0), right_stack(out, 0)
    down, across = iotas()
    for i in (0, 2):
        g = dot(left[:, i * NB : (i + 2) * NB], right[:, : (i + 2) * NB], ((0,), (0,)))

        def block(r, l):
            return g[(r - i) * NB : (r - i + 1) * NB, l * NB : (l + 1) * NB]

        start = i // 2 * PART
        second = block(i + 1, i + 1)
        g_ref[start : start + NB, :] = jnp.where(down >= across, block(i, i), second)
        tail = jnp.sum(jnp.where(down == across, second, 0.0), 0, keepdims=True)
        g_ref[start + 4 * NB : start + PART, :] = jnp.broadcast_to(tail, (PART - 4 * NB, NB))
        for (r, l), (part, n) in PLACES.items():
            if r in (i, i + 1):
                at = part * PART + n * NB
                g_ref[at : at + NB, :] = block(r, l)
    core = core_ref[0]
    keep_ref[...] = g_ref[pl.ds(pl.multiple_of(core * PART, 8), PART), :]
    send_ref[...] = g_ref[pl.ds(pl.multiple_of((1 - core) * PART, 8), PART), :]


def shape(*dims, dtype=F32):
    return jax.ShapeDtypeStruct(dims, dtype)


def call(kernel, outs, specs, name, flops, scratch=()):
    return pl.pallas_call(
        kernel,
        out_shape=outs,
        in_specs=specs,
        out_specs=jax.tree.map(lambda _: VMEM, outs),
        scratch_shapes=scratch,
        compiler_params=pltpu.CompilerParams(vmem_limit_bytes=LIMIT),
        cost_estimate=pl.CostEstimate(flops=flops, bytes_accessed=2**21, transcendentals=0),
        name=name,
    )


NEAR = 3


def lanes(v, k):
    return jnp.broadcast_to(v[:, k : k + 1], (8, NB))


def row(ref, i):
    return jnp.broadcast_to(ref[i : i + 1, :], (8, NB))


def leaf(a, z_ref, d_ref, col_buf, next_buf, a_buf, z_buf, right_buf, left_buf, hook):
    lane = lax.broadcasted_iota(jnp.int32, (8, NB), 1)
    sub = lax.broadcasted_iota(jnp.int32, (8, NB), 0)
    z = [(lane == sub + 8 * r).astype(F32) for r in range(16)]
    diag = jnp.zeros((8, NB), F32)
    for m in range(16):
        k0, p = 8 * m, m % 2
        near = range(m + 1, min(m + 1 + NEAR, 16))
        if m == 0:
            cols = [lanes(a[0], j) for j in range(8)]
        for j in range(8):
            col_buf[p, j] = cols[j]
        a_buf[p] = a[m]
        z_buf[p] = z[m]
        s = {(i, j): row(col_buf.at[p, j], i) for i in range(8) for j in range(i, 8)}
        rb = [row(a_buf.at[p], j) for j in range(8)]
        zb = [row(z_buf.at[p], j) for j in range(8)]
        cr = {r: [lanes(a[r], k0 + j) for j in range(8)] for r in near}
        if m < 15:
            cols = [lanes(a[m + 1], k0 + 8 + j) for j in range(8)]
        for j in range(8):
            inv = 1.0 / s[j, j]
            for jj in range(j + 1, 8):
                f = s[j, jj] * inv
                for k in range(jj, 8):
                    s[jj, k] = s[jj, k] - f * s[j, k]
                rb[jj] = rb[jj] - f * rb[j]
                zb[jj] = zb[jj] - f * zb[j]
            for r in near:
                low = cr[r][j] * inv
                if r == m + 1:
                    next_buf[p, j] = cr[r][j]
                    for jj in range(8):
                        cols[jj] = cols[jj] - low * row(next_buf.at[p, j], jj)
                for jj in range(j + 1, 8):
                    cr[r][jj] = cr[r][jj] - low * s[j, jj]
                a[r] = a[r] - low * rb[j]
                z[r] = z[r] - low * zb[j]
            if m + 1 + NEAR < 16:
                right_buf[p, j : j + 1, :NB] = rb[j][0:1]
                right_buf[p, j : j + 1, NB:] = zb[j][0:1]
                left_buf[p, j : j + 1, :] = (rb[j] * inv)[0:1]
            rs = lax.rsqrt(s[j, j])
            z_ref[k0 + j : k0 + j + 1, :] = (zb[j] * rs)[0:1]
            diag = jnp.where(lane == k0 + j, s[j, j] * rs, diag)
        if m + 1 + NEAR < 16:
            lo = 8 * (m + 1 + NEAR) // 16 * 16
            across = lax.broadcasted_iota(jnp.int32, (NB - lo, NB), 1)
            down = lax.broadcasted_iota(jnp.int32, (NB - lo, NB), 0)
            unit = (across == down + lo).astype(F32).astype(jnp.bfloat16)
            left = dot(unit, left_stack(left_buf[p], 0), ((1,), (1,))).astype(jnp.bfloat16)
            change = dot(left, right_stack(right_buf[p], 0), ((1,), (0,)))
            for r in range(m + 1 + NEAR, 16):
                at = slice(8 * r - lo, 8 * r - lo + 8)
                a[r] = a[r] - change[at, :NB]
                z[r] = z[r] - change[at, NB:]
        hook(m)
    d_ref[...] = diag[0:1]


def finish_kernel(
    root, mine_ref, other_ref, f_ref, core_ref, o_ref, d_ref, w_ref, z_ref, e_ref, *bufs
):
    stored = set()

    def rows(i):
        return slice(i * NB, (i + 1) * NB)

    def get(i, l):
        if (i, l) in stored:
            return w_ref[l, rows(i), :]
        if i >= 4:
            return f_ref[rows(i - 4), rows(l)]
        if i != l:
            part, n = PLACES[i, l]
            return given(part, slice(n * NB, (n + 1) * NB))
        both = given(i // 2, slice(0, NB))
        if i % 2 == 0:
            return jnp.where(down >= across, both, both.T)
        tail = given(i // 2, slice(4 * NB, 4 * NB + 8))[0:1]
        return jnp.where(down == across, tail, jnp.where(down < across, both, both.T))

    def given(part, at):
        return jnp.where(core_ref[0] == part, mine_ref[at, :], other_ref[at, :])

    down, across = iotas()

    def put(i, l, v):
        w_ref[l, rows(i), :] = v
        stored.add((i, l))

    def product(a, b):
        return dot(left_stack(a, 1), right_stack(b, 1), ((1,), (1,)))

    def panel(i, j):
        v = product(get(i, j), z_ref[j])
        put(i, j, v)
        if i >= 4:
            o_ref[rows(i - 4), rows(j)] = (v * root).astype(jnp.bfloat16)

    def update(i, l, j):
        put(i, l, get(i, l) - product(w_ref[j, rows(i), :], w_ref[j, rows(l), :]))

    queue = []

    def hook(_):
        if queue:
            task, where = queue.pop(0)
            task(*where)

    for j in range(4):
        block = get(j, j)
        leaf([block[8 * r : 8 * r + 8] for r in range(16)], z_ref.at[j], e_ref, *bufs, hook)
        d_ref[j : j + 1, :] = e_ref[...] * (1.0 / root)
        while queue:
            hook(j)
        if j < 3:
            panel(j + 1, j)
            update(j + 1, j + 1, j)
        for i in range(j + 2, 4):
            queue.append((panel, (i, j)))
        for i in range(j + 2, 4):
            queue.append((update, (i, j + 1, j)))
        for i in range(j + 2, 4):
            for l in range(j + 2, i + 1):
                queue.append((update, (i, l, j)))
        for i in range(4, 7):
            queue.append((panel, (i, j)))
            for l in range(j + 1, 4):
                queue.append((update, (i, l, j)))
    while queue:
        hook(4)


def exchange(v, axes, count, first):
    pairs = []
    for i in range(first, count - 1, 2):
        pairs += [(i, i + 1), (i + 1, i)]
    return lax.ppermute(v, axes, pairs)


def neighbours(v):
    along_x = exchange(v, GX, 32, 1), exchange(v, GX, 32, 0)
    along_y = exchange(v, GY, 16, 1), exchange(v, GY, 16, 0)
    return along_x, along_y


def swap(v):
    return lax.ppermute(v, "c", [(0, 1), (1, 0)])


def local(initial, couplings, frequencies, linked):
    rows, width = initial.shape[2:]
    v0 = initial[0, 0]
    blocks = couplings[0, 0]
    weights = frequencies[0, 0][:, None]
    present = linked[0, 0]
    core = lax.axis_index("c").astype(jnp.int32)
    odd = lax.rem(lax.axis_index("x"), 2).astype(jnp.int32)
    index = jnp.stack([1 + odd, 2 - odd, 3 + core, 4 - core])
    core = core[None]
    full = shape(rows, width)
    half = shape(rows, width, dtype=jnp.bfloat16)
    flops = 2 * rows * rows * width

    own = call(own_kernel, full, [VMEM] * 3, "own_block", flops)

    pair = shape(rows, 2 * rows, dtype=jnp.bfloat16)
    wide = call(wide_kernel, (pair, pair), [VMEM, SMEM, SMEM], "wide", 1)
    wide_x, wide_y = wide(blocks, present, index)
    specs = [VMEM] * 4
    along_x = call(x_kernel, full, specs, "along_x", 2 * flops)

    def operands(v):
        x_halos, y_halos = neighbours(v)
        part = along_x(own(v, blocks, weights), wide_x, *x_halos)
        return (part, wide_y, *y_halos)

    x1, r1 = call(first_kernel, (full, half), specs, "first", 2 * flops)(*operands(v0))
    r2 = call(middle_kernel, half, specs + [VMEM], "middle", 2 * flops)(*operands(r1), v0)
    piece = shape(PART, NB)
    filtered, keep, send = call(
        last_kernel,
        (full, piece, piece),
        specs + [VMEM, SMEM],
        "last_and_correlation",
        8 * flops,
        (pltpu.VMEM((2 * PART, NB), F32),),
    )(*operands(r2), x1, core)

    summed = keep + swap(send)
    share = PART * NB // 32
    part = lax.all_to_all(summed.reshape(32, share), GX, 0, 0, tiled=True)
    part = part.reshape(32, share).sum(0).reshape(1, share // NB, NB)
    part = lax.all_to_all(jnp.broadcast_to(part, (8, share // NB, NB)), "y", 0, 0)
    total = part.sum(0).reshape(1, share)
    mine = lax.all_to_all(jnp.broadcast_to(total, (32, share)), GX, 0, 0, tiled=True)
    mine = mine.reshape(PART, NB)
    other = swap(mine)

    root = math.sqrt(rows * 512)
    out, diag = call(
        functools.partial(finish_kernel, root),
        (half, shape(4, NB)),
        [VMEM] * 3 + [SMEM],
        "finish",
        8 * flops,
        (
            pltpu.VMEM((4, width + rows, NB), F32),
            pltpu.VMEM((4, NB, NB), F32),
            pltpu.VMEM((1, NB), F32),
            pltpu.VMEM((2, 8, 8, NB), F32),
            pltpu.VMEM((2, 8, 8, NB), F32),
            pltpu.VMEM((2, 8, NB), F32),
            pltpu.VMEM((2, 8, NB), F32),
            pltpu.VMEM((2, 8, 2 * NB), F32),
            pltpu.VMEM((2, 8, NB), F32),
        ),
    )(mine, other, filtered, core)
    return out[None, None], diag.reshape(width)


def solution(mesh):
    fine = Mesh(mesh.devices.reshape(8, 4, 8, 2), GX + GY)
    in_specs = (
        P(GX, GY, None, None),
        P(GX, GY, None, None, None),
        P(GX, GY, None),
        P(GX, GY, None),
    )
    out_specs = (P(GX, GY, None, None), P())
    return jax.shard_map(local, mesh=fine, in_specs=in_specs, out_specs=out_specs, check_vma=False)
```

```python
import functools
import math

import jax
import jax.numpy as jnp
from jax import lax
from jax.experimental import pallas as pl
from jax.experimental.pallas import tpu as pltpu
from jax.sharding import Mesh
from jax.sharding import PartitionSpec as P

CENTER = 1.25
SCALE = 0.5
NB = 128
F32 = jnp.float32
VMEM = pl.BlockSpec(memory_space=pltpu.VMEM)
SMEM = pl.BlockSpec(memory_space=pltpu.SMEM)
GX = ("z", "x")
GY = ("y", "c")
LIMIT = 12 * 2**20
PART = 4 * NB + 32
PLACES = {(1, 0): (0, 1), (2, 0): (0, 2), (3, 0): (0, 3), (2, 1): (1, 1), (3, 1): (1, 2), (3, 2): (1, 3)}


def iotas():
    return [lax.broadcasted_iota(jnp.int32, (NB, NB), d) for d in (0, 1)]


def dot(a, b, dims):
    return lax.dot_general(a, b, (dims, ((), ())), preferred_element_type=F32)


def wide_kernel(c_ref, l_ref, i_ref, own_ref, x_ref, y_ref):
    own_ref[...] = c_ref[0]
    none = jnp.zeros(c_ref.shape[1:], c_ref.dtype)
    for k in range(4):
        index = i_ref[k]
        at = slice(k % 2 * none.shape[1], (k % 2 + 1) * none.shape[1])
        (x_ref if k < 2 else y_ref)[:, at] = jnp.where(l_ref[index - 1] != 0, c_ref[index], none)


def halo_sum(part_ref, wide_ref, h0, h1):
    halos = jnp.concatenate([h0[...], h1[...]], 0)
    return part_ref[...] + dot(wide_ref[...], halos, ((1,), (0,)))


def own_kernel(v_ref, c_ref, w_ref, o_ref):
    v = v_ref[...]
    o_ref[...] = (w_ref[...] - CENTER) * v.astype(F32) + dot(c_ref[...], v, ((1,), (0,)))


def x_kernel(part_ref, wide_ref, h0, h1, o_ref):
    o_ref[...] = halo_sum(part_ref, wide_ref, h0, h1)


def first_kernel(part_ref, wide_ref, h0, h1, o_ref, r_ref):
    out = SCALE * halo_sum(part_ref, wide_ref, h0, h1)
    o_ref[...] = out
    r_ref[...] = out.astype(jnp.bfloat16)


def middle_kernel(part_ref, wide_ref, h0, h1, p_ref, r_ref):
    total = halo_sum(part_ref, wide_ref, h0, h1)
    r_ref[...] = (2.0 * SCALE * total - p_ref[...].astype(F32)).astype(jnp.bfloat16)


def split(v):
    high = v.astype(jnp.bfloat16).astype(F32)
    rest = v - high
    middle = rest.astype(jnp.bfloat16).astype(F32)
    return high, middle, rest - middle


def stack(parts, axis):
    return jnp.concatenate(parts, axis).astype(jnp.bfloat16)


def left_stack(v, axis):
    high, middle, low = split(v)
    return stack([low, high, middle, middle, high, high], axis)


def right_stack(v, axis):
    high, middle, low = split(v)
    return stack([high, low, middle, high, middle, high], axis)


def last_kernel(part_ref, wide_ref, h0, h1, p_ref, core_ref, o_ref, keep_ref, send_ref, g_ref):
    out = 2.0 * SCALE * halo_sum(part_ref, wide_ref, h0, h1) - p_ref[...]
    o_ref[...] = out
    left, right = left_stack(out, 0), right_stack(out, 0)
    down, across = iotas()
    for i in (0, 2):
        g = dot(left[:, i * NB : (i + 2) * NB], right[:, : (i + 2) * NB], ((0,), (0,)))

        def block(r, l):
            return g[(r - i) * NB : (r - i + 1) * NB, l * NB : (l + 1) * NB]

        start = i // 2 * PART
        second = block(i + 1, i + 1)
        g_ref[start : start + NB, :] = jnp.where(down >= across, block(i, i), second)
        tail = jnp.sum(jnp.where(down == across, second, 0.0), 0, keepdims=True)
        g_ref[start + 4 * NB : start + PART, :] = jnp.broadcast_to(tail, (PART - 4 * NB, NB))
        for (r, l), (part, n) in PLACES.items():
            if r in (i, i + 1):
                at = part * PART + n * NB
                g_ref[at : at + NB, :] = block(r, l)
    core = core_ref[0]
    keep_ref[...] = g_ref[pl.ds(pl.multiple_of(core * PART, 8), PART), :]
    send_ref[...] = g_ref[pl.ds(pl.multiple_of((1 - core) * PART, 8), PART), :]


def shape(*dims, dtype=F32):
    return jax.ShapeDtypeStruct(dims, dtype)


def call(kernel, outs, specs, name, flops, scratch=()):
    return pl.pallas_call(
        kernel,
        out_shape=outs,
        in_specs=specs,
        out_specs=jax.tree.map(lambda _: VMEM, outs),
        scratch_shapes=scratch,
        compiler_params=pltpu.CompilerParams(vmem_limit_bytes=LIMIT),
        cost_estimate=pl.CostEstimate(flops=flops, bytes_accessed=2**21, transcendentals=0),
        name=name,
    )


NEAR = 3


def lanes(v, k):
    return jnp.broadcast_to(v[:, k : k + 1], (8, NB))


def row(ref, i):
    return jnp.broadcast_to(ref[i : i + 1, :], (8, NB))


def leaf(a, z_ref, d_ref, col_buf, next_buf, a_buf, z_buf, right_buf, left_buf, hook):
    lane = lax.broadcasted_iota(jnp.int32, (8, NB), 1)
    sub = lax.broadcasted_iota(jnp.int32, (8, NB), 0)
    z = [(lane == sub + 8 * r).astype(F32) for r in range(16)]
    diag = jnp.zeros((8, NB), F32)
    for m in range(16):
        k0, p = 8 * m, m % 2
        near = range(m + 1, min(m + 1 + NEAR, 16))
        if m == 0:
            cols = [lanes(a[0], j) for j in range(8)]
        for j in range(8):
            col_buf[p, j] = cols[j]
        a_buf[p] = a[m]
        z_buf[p] = z[m]
        s = {(i, j): row(col_buf.at[p, j], i) for i in range(8) for j in range(i, 8)}
        rb = [row(a_buf.at[p], j) for j in range(8)]
        zb = [row(z_buf.at[p], j) for j in range(8)]
        cr = {r: [lanes(a[r], k0 + j) for j in range(8)] for r in near}
        if m < 15:
            cols = [lanes(a[m + 1], k0 + 8 + j) for j in range(8)]
        for j in range(8):
            inv = 1.0 / s[j, j]
            for jj in range(j + 1, 8):
                f = s[j, jj] * inv
                for k in range(jj, 8):
                    s[jj, k] = s[jj, k] - f * s[j, k]
                rb[jj] = rb[jj] - f * rb[j]
                zb[jj] = zb[jj] - f * zb[j]
            for r in near:
                low = cr[r][j] * inv
                if r == m + 1:
                    next_buf[p, j] = cr[r][j]
                    for jj in range(8):
                        cols[jj] = cols[jj] - low * row(next_buf.at[p, j], jj)
                for jj in range(j + 1, 8):
                    cr[r][jj] = cr[r][jj] - low * s[j, jj]
                a[r] = a[r] - low * rb[j]
                z[r] = z[r] - low * zb[j]
            if m + 1 + NEAR < 16:
                right_buf[p, j : j + 1, :NB] = rb[j][0:1]
                right_buf[p, j : j + 1, NB:] = zb[j][0:1]
                left_buf[p, j : j + 1, :] = (rb[j] * inv)[0:1]
            rs = lax.rsqrt(s[j, j])
            z_ref[k0 + j : k0 + j + 1, :] = (zb[j] * rs)[0:1]
            diag = jnp.where(lane == k0 + j, s[j, j] * rs, diag)
        if m + 1 + NEAR < 16:
            lo = 8 * (m + 1 + NEAR) // 16 * 16
            across = lax.broadcasted_iota(jnp.int32, (NB - lo, NB), 1)
            down = lax.broadcasted_iota(jnp.int32, (NB - lo, NB), 0)
            unit = (across == down + lo).astype(F32).astype(jnp.bfloat16)
            left = dot(unit, left_stack(left_buf[p], 0), ((1,), (1,))).astype(jnp.bfloat16)
            change = dot(left, right_stack(right_buf[p], 0), ((1,), (0,)))
            for r in range(m + 1 + NEAR, 16):
                at = slice(8 * r - lo, 8 * r - lo + 8)
                a[r] = a[r] - change[at, :NB]
                z[r] = z[r] - change[at, NB:]
        hook(m)
    d_ref[...] = diag[0:1]


def finish_kernel(
    root, mine_ref, other_ref, f_ref, core_ref, o_ref, d_ref, w_ref, z_ref, e_ref, *bufs
):
    stored = set()

    def rows(i):
        return slice(i * NB, (i + 1) * NB)

    def get(i, l):
        if (i, l) in stored:
            return w_ref[l, rows(i), :]
        if i >= 4:
            return f_ref[rows(i - 4), rows(l)]
        if i != l:
            part, n = PLACES[i, l]
            return given(part, slice(n * NB, (n + 1) * NB))
        both = given(i // 2, slice(0, NB))
        if i % 2 == 0:
            return jnp.where(down >= across, both, both.T)
        tail = given(i // 2, slice(4 * NB, 4 * NB + 8))[0:1]
        return jnp.where(down == across, tail, jnp.where(down < across, both, both.T))

    def given(part, at):
        return jnp.where(core_ref[0] == part, mine_ref[at, :], other_ref[at, :])

    down, across = iotas()

    def put(i, l, v):
        w_ref[l, rows(i), :] = v
        stored.add((i, l))

    def product(a, b):
        return dot(left_stack(a, 1), right_stack(b, 1), ((1,), (1,)))

    def panel(i, j):
        v = product(get(i, j), z_ref[j])
        put(i, j, v)
        if i >= 4:
            o_ref[rows(i - 4), rows(j)] = (v * root).astype(jnp.bfloat16)

    def update(i, l, j):
        put(i, l, get(i, l) - product(w_ref[j, rows(i), :], w_ref[j, rows(l), :]))

    queue = []

    def hook(_):
        if queue:
            task, where = queue.pop(0)
            task(*where)

    for j in range(4):
        block = get(j, j)
        leaf([block[8 * r : 8 * r + 8] for r in range(16)], z_ref.at[j], e_ref, *bufs, hook)
        d_ref[j : j + 1, :] = e_ref[...] * (1.0 / root)
        while queue:
            hook(j)
        if j < 3:
            panel(j + 1, j)
            update(j + 1, j + 1, j)
        for i in range(j + 2, 4):
            queue.append((panel, (i, j)))
        for i in range(j + 2, 4):
            queue.append((update, (i, j + 1, j)))
        for i in range(j + 2, 4):
            for l in range(j + 2, i + 1):
                queue.append((update, (i, l, j)))
        for i in range(4, 7):
            queue.append((panel, (i, j)))
            for l in range(j + 1, 4):
                queue.append((update, (i, l, j)))
    while queue:
        hook(4)


def exchange(v, axes, count, first):
    pairs = []
    for i in range(first, count - 1, 2):
        pairs += [(i, i + 1), (i + 1, i)]
    return lax.ppermute(v, axes, pairs)


def neighbours(v):
    along_x = exchange(v, GX, 32, 1), exchange(v, GX, 32, 0)
    along_y = exchange(v, GY, 16, 1), exchange(v, GY, 16, 0)
    return along_x, along_y


def swap(v):
    return lax.ppermute(v, "c", [(0, 1), (1, 0)])


def local(initial, couplings, frequencies, linked):
    rows, width = initial.shape[2:]
    v0 = initial[0, 0]
    blocks = couplings[0, 0]
    weights = frequencies[0, 0][:, None]
    present = linked[0, 0]
    core = lax.axis_index("c").astype(jnp.int32)
    odd = lax.rem(lax.axis_index("x"), 2).astype(jnp.int32)
    index = jnp.stack([1 + odd, 2 - odd, 3 + core, 4 - core])
    core = core[None]
    full = shape(rows, width)
    half = shape(rows, width, dtype=jnp.bfloat16)
    flops = 2 * rows * rows * width

    own = call(own_kernel, full, [VMEM] * 3, "own_block", flops)

    pair = shape(rows, 2 * rows, dtype=jnp.bfloat16)
    square = shape(rows, rows, dtype=jnp.bfloat16)
    wide = call(wide_kernel, (square, pair, pair), [VMEM, SMEM, SMEM], "wide", flops)
    block, wide_x, wide_y = wide(blocks, present, index)
    specs = [VMEM] * 4
    along_x = call(x_kernel, full, specs, "along_x", 2 * flops)

    def operands(v):
        x_halos, y_halos = neighbours(v)
        part = along_x(own(v, block, weights), wide_x, *x_halos)
        return (part, wide_y, *y_halos)

    x1, r1 = call(first_kernel, (full, half), specs, "first", 2 * flops)(*operands(v0))
    r2 = call(middle_kernel, half, specs + [VMEM], "middle", 2 * flops)(*operands(r1), v0)
    piece = shape(PART, NB)
    filtered, keep, send = call(
        last_kernel,
        (full, piece, piece),
        specs + [VMEM, SMEM],
        "last_and_correlation",
        8 * flops,
        (pltpu.VMEM((2 * PART, NB), F32),),
    )(*operands(r2), x1, core)

    summed = keep + swap(send)
    share = PART * NB // 32
    part = lax.all_to_all(summed.reshape(32, share), GX, 0, 0, tiled=True)
    part = part.reshape(32, share).sum(0).reshape(1, share // NB, NB)
    part = lax.all_to_all(jnp.broadcast_to(part, (8, share // NB, NB)), "y", 0, 0)
    total = part.sum(0).reshape(1, share)
    mine = lax.all_to_all(jnp.broadcast_to(total, (32, share)), GX, 0, 0, tiled=True)
    mine = mine.reshape(PART, NB)
    other = swap(mine)

    root = math.sqrt(rows * 512)
    out, diag = call(
        functools.partial(finish_kernel, root),
        (half, shape(4, NB)),
        [VMEM] * 3 + [SMEM],
        "finish",
        8 * flops,
        (
            pltpu.VMEM((4, width + rows, NB), F32),
            pltpu.VMEM((4, NB, NB), F32),
            pltpu.VMEM((1, NB), F32),
            pltpu.VMEM((2, 8, 8, NB), F32),
            pltpu.VMEM((2, 8, 8, NB), F32),
            pltpu.VMEM((2, 8, NB), F32),
            pltpu.VMEM((2, 8, NB), F32),
            pltpu.VMEM((2, 8, 2 * NB), F32),
            pltpu.VMEM((2, 8, NB), F32),
        ),
    )(mine, other, filtered, core)
    return out[None, None], diag.reshape(width)


def solution(mesh):
    fine = Mesh(mesh.devices.reshape(8, 4, 8, 2), GX + GY)
    in_specs = (
        P(GX, GY, None, None),
        P(GX, GY, None, None, None),
        P(GX, GY, None),
        P(GX, GY, None),
    )
    out_specs = (P(GX, GY, None, None), P())
    return jax.shard_map(local, mesh=fine, in_specs=in_specs, out_specs=out_specs, check_vma=False)
```

```python
import functools
import math

import jax
import jax.numpy as jnp
from jax import lax
from jax.experimental import pallas as pl
from jax.experimental.pallas import tpu as pltpu
from jax.sharding import Mesh
from jax.sharding import PartitionSpec as P

CENTER = 1.25
SCALE = 0.5
NB = 128
F32 = jnp.float32
VMEM = pl.BlockSpec(memory_space=pltpu.VMEM)
SMEM = pl.BlockSpec(memory_space=pltpu.SMEM)
GX = ("z", "x")
GY = ("y", "c")
LIMIT = 12 * 2**20
PART = 4 * NB + 32
PLACES = {(1, 0): (0, 1), (2, 0): (0, 2), (3, 0): (0, 3), (2, 1): (1, 1), (3, 1): (1, 2), (3, 2): (1, 3)}


def iotas():
    return [lax.broadcasted_iota(jnp.int32, (NB, NB), d) for d in (0, 1)]


def dot(a, b, dims):
    return lax.dot_general(a, b, (dims, ((), ())), preferred_element_type=F32)


def wide_kernel(c_ref, l_ref, i_ref, own_ref, x_ref, y_ref):
    own_ref[...] = c_ref[0]
    none = jnp.zeros(c_ref.shape[1:], c_ref.dtype)
    for k in range(4):
        index = i_ref[k]
        at = slice(k % 2 * none.shape[1], (k % 2 + 1) * none.shape[1])
        (x_ref if k < 2 else y_ref)[:, at] = jnp.where(l_ref[index - 1] != 0, c_ref[index], none)


def halo_sum(part_ref, wide_ref, h0, h1):
    halos = jnp.concatenate([h0[...], h1[...]], 0)
    return part_ref[...] + dot(wide_ref[...], halos, ((1,), (0,)))


def own_kernel(v_ref, c_ref, w_ref, o_ref):
    v = v_ref[...]
    o_ref[...] = (w_ref[...] - CENTER) * v.astype(F32) + dot(c_ref[...], v, ((1,), (0,)))


def x_kernel(part_ref, wide_ref, h0, h1, o_ref):
    o_ref[...] = halo_sum(part_ref, wide_ref, h0, h1)


def first_kernel(part_ref, wide_ref, h0, h1, o_ref, r_ref):
    out = SCALE * halo_sum(part_ref, wide_ref, h0, h1)
    o_ref[...] = out
    r_ref[...] = out.astype(jnp.bfloat16)


def middle_kernel(part_ref, wide_ref, h0, h1, p_ref, r_ref):
    total = halo_sum(part_ref, wide_ref, h0, h1)
    r_ref[...] = (2.0 * SCALE * total - p_ref[...].astype(F32)).astype(jnp.bfloat16)


def split(v):
    high = v.astype(jnp.bfloat16).astype(F32)
    rest = v - high
    middle = rest.astype(jnp.bfloat16).astype(F32)
    return high, middle, rest - middle


def stack(parts, axis):
    return jnp.concatenate(parts, axis).astype(jnp.bfloat16)


def left_stack(v, axis):
    high, middle, low = split(v)
    return stack([low, high, middle, middle, high, high], axis)


def right_stack(v, axis):
    high, middle, low = split(v)
    return stack([high, low, middle, high, middle, high], axis)


def last_kernel(part_ref, wide_ref, h0, h1, p_ref, core_ref, o_ref, keep_ref, send_ref, g_ref):
    out = 2.0 * SCALE * halo_sum(part_ref, wide_ref, h0, h1) - p_ref[...]
    o_ref[...] = out
    left, right = left_stack(out, 0), right_stack(out, 0)
    down, across = iotas()
    for i in (0, 2):
        g = dot(left[:, i * NB : (i + 2) * NB], right[:, : (i + 2) * NB], ((0,), (0,)))

        def block(r, l):
            return g[(r - i) * NB : (r - i + 1) * NB, l * NB : (l + 1) * NB]

        start = i // 2 * PART
        second = block(i + 1, i + 1)
        g_ref[start : start + NB, :] = jnp.where(down >= across, block(i, i), second)
        tail = jnp.sum(jnp.where(down == across, second, 0.0), 0, keepdims=True)
        g_ref[start + 4 * NB : start + PART, :] = jnp.broadcast_to(tail, (PART - 4 * NB, NB))
        for (r, l), (part, n) in PLACES.items():
            if r in (i, i + 1):
                at = part * PART + n * NB
                g_ref[at : at + NB, :] = block(r, l)
    core = core_ref[0]
    keep_ref[...] = g_ref[pl.ds(pl.multiple_of(core * PART, 8), PART), :]
    send_ref[...] = g_ref[pl.ds(pl.multiple_of((1 - core) * PART, 8), PART), :]


def shape(*dims, dtype=F32):
    return jax.ShapeDtypeStruct(dims, dtype)


def call(kernel, outs, specs, name, flops, scratch=()):
    return pl.pallas_call(
        kernel,
        out_shape=outs,
        in_specs=specs,
        out_specs=jax.tree.map(lambda _: VMEM, outs),
        scratch_shapes=scratch,
        compiler_params=pltpu.CompilerParams(vmem_limit_bytes=LIMIT),
        cost_estimate=pl.CostEstimate(flops=flops, bytes_accessed=2**21, transcendentals=0),
        name=name,
    )


NEAR = 3


def lanes(v, k):
    return jnp.broadcast_to(v[:, k : k + 1], (8, NB))


def row(ref, i):
    return jnp.broadcast_to(ref[i : i + 1, :], (8, NB))


def leaf(a, z_ref, d_ref, col_buf, next_buf, a_buf, z_buf, right_buf, left_buf, hook):
    lane = lax.broadcasted_iota(jnp.int32, (8, NB), 1)
    sub = lax.broadcasted_iota(jnp.int32, (8, NB), 0)
    z = [(lane == sub + 8 * r).astype(F32) for r in range(16)]
    diag = jnp.zeros((8, NB), F32)
    for m in range(16):
        k0, p = 8 * m, m % 2
        near = range(m + 1, min(m + 1 + NEAR, 16))
        if m == 0:
            cols = [lanes(a[0], j) for j in range(8)]
        for j in range(8):
            col_buf[p, j] = cols[j]
        a_buf[p] = a[m]
        z_buf[p] = z[m]
        s = {(i, j): row(col_buf.at[p, j], i) for i in range(8) for j in range(i, 8)}
        rb = [row(a_buf.at[p], j) for j in range(8)]
        zb = [row(z_buf.at[p], j) for j in range(8)]
        cr = {r: [lanes(a[r], k0 + j) for j in range(8)] for r in near}
        if m < 15:
            cols = [lanes(a[m + 1], k0 + 8 + j) for j in range(8)]
        for j in range(8):
            inv = 1.0 / s[j, j]
            for jj in range(j + 1, 8):
                f = s[j, jj] * inv
                for k in range(jj, 8):
                    s[jj, k] = s[jj, k] - f * s[j, k]
                rb[jj] = rb[jj] - f * rb[j]
                zb[jj] = zb[jj] - f * zb[j]
            for r in near:
                low = cr[r][j] * inv
                if r == m + 1:
                    next_buf[p, j] = cr[r][j]
                    for jj in range(8):
                        cols[jj] = cols[jj] - low * row(next_buf.at[p, j], jj)
                for jj in range(j + 1, 8):
                    cr[r][jj] = cr[r][jj] - low * s[j, jj]
                a[r] = a[r] - low * rb[j]
                z[r] = z[r] - low * zb[j]
            if m + 1 + NEAR < 16:
                right_buf[p, j : j + 1, :NB] = rb[j][0:1]
                right_buf[p, j : j + 1, NB:] = zb[j][0:1]
                left_buf[p, j : j + 1, :] = (rb[j] * inv)[0:1]
            rs = lax.rsqrt(s[j, j])
            z_ref[k0 + j : k0 + j + 1, :] = (zb[j] * rs)[0:1]
            diag = jnp.where(lane == k0 + j, s[j, j] * rs, diag)
        if m + 1 + NEAR < 16:
            lo = 8 * (m + 1 + NEAR) // 16 * 16
            across = lax.broadcasted_iota(jnp.int32, (NB - lo, NB), 1)
            down = lax.broadcasted_iota(jnp.int32, (NB - lo, NB), 0)
            unit = (across == down + lo).astype(F32).astype(jnp.bfloat16)
            left = dot(unit, left_stack(left_buf[p], 0), ((1,), (1,))).astype(jnp.bfloat16)
            change = dot(left, right_stack(right_buf[p], 0), ((1,), (0,)))
            for r in range(m + 1 + NEAR, 16):
                at = slice(8 * r - lo, 8 * r - lo + 8)
                a[r] = a[r] - change[at, :NB]
                z[r] = z[r] - change[at, NB:]
        hook(m)
    d_ref[...] = diag[0:1]


def finish_kernel(
    root, mine_ref, other_ref, f_ref, core_ref, o_ref, d_ref, w_ref, z_ref, e_ref, *bufs
):
    stored = set()

    def rows(i):
        return slice(i * NB, (i + 1) * NB)

    def get(i, l):
        if (i, l) in stored:
            return w_ref[l, rows(i), :]
        if i >= 4:
            return f_ref[rows(i - 4), rows(l)]
        if i != l:
            part, n = PLACES[i, l]
            return given(part, slice(n * NB, (n + 1) * NB))
        both = given(i // 2, slice(0, NB))
        if i % 2 == 0:
            return jnp.where(down >= across, both, both.T)
        tail = given(i // 2, slice(4 * NB, 4 * NB + 8))[0:1]
        return jnp.where(down == across, tail, jnp.where(down < across, both, both.T))

    def given(part, at):
        return jnp.where(core_ref[0] == part, mine_ref[at, :], other_ref[at, :])

    down, across = iotas()

    def put(i, l, v):
        w_ref[l, rows(i), :] = v
        stored.add((i, l))

    def product(a, b):
        return dot(left_stack(a, 1), right_stack(b, 1), ((1,), (1,)))

    def panel(i, j):
        v = product(get(i, j), z_ref[j])
        put(i, j, v)
        if i >= 4:
            o_ref[rows(i - 4), rows(j)] = (v * root).astype(jnp.bfloat16)

    def update(i, l, j):
        put(i, l, get(i, l) - product(w_ref[j, rows(i), :], w_ref[j, rows(l), :]))

    queue = []

    def hook(_):
        if queue:
            task, where = queue.pop(0)
            task(*where)

    for j in range(4):
        block = get(j, j)
        leaf([block[8 * r : 8 * r + 8] for r in range(16)], z_ref.at[j], e_ref, *bufs, hook)
        d_ref[j : j + 1, :] = e_ref[...] * (1.0 / root)
        while queue:
            hook(j)
        if j < 3:
            panel(j + 1, j)
            update(j + 1, j + 1, j)
        for i in range(j + 2, 4):
            queue.append((panel, (i, j)))
        for i in range(j + 2, 4):
            queue.append((update, (i, j + 1, j)))
        for i in range(j + 2, 4):
            for l in range(j + 2, i + 1):
                queue.append((update, (i, l, j)))
        for i in range(4, 7):
            queue.append((panel, (i, j)))
            for l in range(j + 1, 4):
                queue.append((update, (i, l, j)))
    while queue:
        hook(4)


def exchange(v, axes, count, first):
    pairs = []
    for i in range(first, count - 1, 2):
        pairs += [(i, i + 1), (i + 1, i)]
    return lax.ppermute(v, axes, pairs)


def neighbours(v):
    along_x = exchange(v, GX, 32, 1), exchange(v, GX, 32, 0)
    along_y = exchange(v, GY, 16, 1), exchange(v, GY, 16, 0)
    return along_x, along_y


def swap(v):
    return lax.ppermute(v, "c", [(0, 1), (1, 0)])


def local(initial, couplings, frequencies, linked):
    rows, width = initial.shape[2:]
    v0 = initial[0, 0]
    blocks = couplings[0, 0]
    weights = frequencies[0, 0][:, None]
    present = linked[0, 0]
    core = lax.axis_index("c").astype(jnp.int32)
    odd = lax.rem(lax.axis_index("x"), 2).astype(jnp.int32)
    index = jnp.stack([1 + odd, 2 - odd, 3 + core, 4 - core])
    core = core[None]
    full = shape(rows, width)
    half = shape(rows, width, dtype=jnp.bfloat16)
    flops = 2 * rows * rows * width

    own = call(own_kernel, full, [VMEM] * 3, "own_block", flops)

    pair = shape(rows, 2 * rows, dtype=jnp.bfloat16)
    square = shape(rows, rows, dtype=jnp.bfloat16)
    wide = call(wide_kernel, (square, pair, pair), [VMEM, SMEM, SMEM], "wide", flops)
    block, wide_x, wide_y = wide(blocks, present, index)
    specs = [VMEM] * 4
    along_x = call(x_kernel, full, specs, "along_x", 2 * flops)

    def operands(v):
        x_halos, y_halos = neighbours(v)
        part = along_x(own(v, block, weights), wide_x, *x_halos)
        return (part, wide_y, *y_halos)

    x1, r1 = call(first_kernel, (full, half), specs, "first", 2 * flops)(*operands(v0))
    r2 = call(middle_kernel, half, specs + [VMEM], "middle", 2 * flops)(*operands(r1), v0)
    piece = shape(PART, NB)
    filtered, keep, send = call(
        last_kernel,
        (full, piece, piece),
        specs + [VMEM, SMEM],
        "last_and_correlation",
        8 * flops,
        (pltpu.VMEM((2 * PART, NB), F32),),
    )(*operands(r2), x1, core)

    summed = keep + swap(send)
    share = PART * NB // 32
    part = lax.all_to_all(summed.reshape(32, share), GX, 0, 0, tiled=True)
    part = part.reshape(32, share).sum(0, keepdims=True)
    part = lax.all_to_all(jnp.broadcast_to(part, (8, share)), "y", 0, 0, tiled=True)
    total = part.reshape(8, share).sum(0, keepdims=True)
    mine = lax.all_to_all(jnp.broadcast_to(total, (32, share)), GX, 0, 0, tiled=True)
    mine = mine.reshape(PART, NB)
    other = swap(mine)

    root = math.sqrt(rows * 512)
    out, diag = call(
        functools.partial(finish_kernel, root),
        (half, shape(4, NB)),
        [VMEM] * 3 + [SMEM],
        "finish",
        8 * flops,
        (
            pltpu.VMEM((4, width + rows, NB), F32),
            pltpu.VMEM((4, NB, NB), F32),
            pltpu.VMEM((1, NB), F32),
            pltpu.VMEM((2, 8, 8, NB), F32),
            pltpu.VMEM((2, 8, 8, NB), F32),
            pltpu.VMEM((2, 8, NB), F32),
            pltpu.VMEM((2, 8, NB), F32),
            pltpu.VMEM((2, 8, 2 * NB), F32),
            pltpu.VMEM((2, 8, NB), F32),
        ),
    )(mine, other, filtered, core)
    return out[None, None], diag.reshape(width)


def solution(mesh):
    fine = Mesh(mesh.devices.reshape(8, 4, 8, 2), GX + GY)
    in_specs = (
        P(GX, GY, None, None),
        P(GX, GY, None, None, None),
        P(GX, GY, None),
        P(GX, GY, None),
    )
    out_specs = (P(GX, GY, None, None), P())
    return jax.shard_map(local, mesh=fine, in_specs=in_specs, out_specs=out_specs, check_vma=False)
```
